32 devices in a mesh: blk: 8 (over y, x, core), rep: 4 (over z).
Axes of the slice: x: 2, y: 2, z: 4, core: 2. Of those that a mesh axis runs over, the one named last changes fastest.
Arguments:
- point_pool: bfloat16 [40960, 1024], P(('blk', 'rep')), may hold values from -8 to 8
- batch_rows: int32 [32768], P(('blk', 'rep')), may hold values from 0 to 1279
- targets: bfloat16 [32768, 256], P(('blk', 'rep')), may hold values from -6 to 6
- center_pool: bfloat16 [512, 1024], P('blk'), may hold values from -8 to 8
- center_rows: int32 [256], P('blk'), may hold values from 0 to 63
- coefs: bfloat16 [256, 256], P('blk'), may hold values from -3 to 3
Outputs:
- residual: float32 [32768, 256], P(('blk', 'rep'))
- coef_grad: float32 [256, 256], P('blk')
The draws below stay inside these ranges and needn't reach their ends.
All inputs are finite; a program needn't handle non-finite values.
Results may differ from the reference program's by a relative error of at most 0.0016.
Values may be sent and summed in bfloat16 or wider, within the bound.
No kernel may reach another device: no remote copies, remote signals or barrier semaphores. Data moves between devices by JAX's collectives and lax.ppermute only.
A program may use at most 64 MiB of HBM per device.

```python
import jax
import jax.numpy as jnp
from jax import lax

D = 1024
OUTS = 256
PTS_DEV = 1024
CEN_DEV = 32
POOL_DEV = 1280
CPOOL_DEV = 64
POINTS = 32768
POOL = 40960
CENTERS = 256
CPOOL = 512


def shared_rows(key, row_count, stream_id):
    latent_dims = 16
    mixing = jax.random.normal(jax.random.fold_in(key, 101), (latent_dims, D), jnp.float32)
    spread = 0.245
    jitter = 0.3 * jax.random.normal(jax.random.fold_in(key, stream_id + 1), (row_count, D), jnp.float32)
    latent = spread * jax.random.normal(jax.random.fold_in(key, stream_id), (row_count, latent_dims), jnp.float32)
    result_rows = jnp.dot(latent, mixing, precision=lax.Precision.HIGHEST) + jitter
    return jnp.clip(result_rows, -8.0, 8.0)


def draw_point_pool(key, part):
    return shared_rows(key, POOL, 211).astype(jnp.bfloat16)


def draw_center_pool(key, part):
    return shared_rows(key, CPOOL, 307).astype(jnp.bfloat16)


def draw_targets(key, part):
    block_count = POINTS // PTS_DEV
    shifts = jax.random.uniform(jax.random.fold_in(key, 401), (block_count, 1, 1), jnp.float32, 0.0, 3.0)
    noise = jax.random.normal(jax.random.fold_in(key, 405), (block_count, PTS_DEV, OUTS), jnp.float32)
    values = jnp.clip(noise + shifts, -6.0, 6.0)
    return values.reshape(POINTS, OUTS).astype(jnp.bfloat16)


def touch_ends(result, key, smallest, largest):
    extent = result.shape
    place = [jax.random.randint(jax.random.fold_in(key, axis), (), 0, extent[axis]) for axis in range(len(extent))]
    result = result.at[tuple(place)].set(smallest)
    longest = extent.index(max(extent))
    place[longest] = (place[longest] + 1) % extent[longest]
    return result.at[tuple(place)].set(largest)


def steps_of(key, shape, split, low, top_value):
    factor_of = 1.0
    for dim, blocks in split:
        draws = jax.random.uniform(jax.random.fold_in(jax.random.fold_in(key, 6), dim), (blocks,), jnp.float32, low / len(split), top_value / len(split))
        factor_of = factor_of * jnp.repeat(jnp.exp(draws), shape[dim] // blocks).reshape((-1,) + (1,) * (len(shape) - 1 - dim))
    return factor_of


def scatter_about(stream_key, dims, scale, most, cuts=(), kind=jnp.bfloat16):
    gain = steps_of(stream_key, dims, cuts, -0.22, 0.18) if cuts else 1.0
    values = jax.random.normal(stream_key, dims, jnp.float32) * scale * gain
    return jnp.minimum(jnp.maximum(values, -most), most).astype(kind)


def setup_inputs(seed: int = 0) -> dict:
    arg_keys = jax.random.split(jax.random.key(seed), 7)
    point_pool = draw_point_pool(jax.random.fold_in(arg_keys[6], 71), 0)
    batch_rows = touch_ends(jax.random.randint(arg_keys[1], (POINTS,), 0, POOL_DEV), jax.random.fold_in(arg_keys[1], 1), 0, POOL_DEV - 1).astype(jnp.int32)
    targets = draw_targets(jax.random.fold_in(arg_keys[6], 71), 0)
    center_pool = draw_center_pool(jax.random.fold_in(arg_keys[6], 71), 0)
    center_rows = touch_ends(jax.random.randint(arg_keys[4], (CENTERS,), 0, CPOOL_DEV), jax.random.fold_in(arg_keys[4], 1), 0, CPOOL_DEV - 1).astype(jnp.int32)
    coefs = scatter_about(arg_keys[5], (CENTERS, OUTS), (max(CENTERS // 55, 1)) ** -0.5, 3.0, ((0, 8),))
    return {"point_pool": point_pool, "batch_rows": batch_rows, "targets": targets, "center_pool": center_pool, "center_rows": center_rows, "coefs": coefs}


def reference(point_pool, batch_rows, targets, center_pool, center_rows, coefs):
    owner = jnp.arange(POINTS, dtype=jnp.int32) // PTS_DEV
    points = jnp.take(point_pool, (owner * POOL_DEV + batch_rows).astype(jnp.int32), axis=0)
    center_owner = jnp.arange(CENTERS, dtype=jnp.int32) // CEN_DEV
    centers = jnp.take(center_pool, (center_owner * CPOOL_DEV + center_rows).astype(jnp.int32), axis=0)
    center_norm = jnp.sum(centers.astype(jnp.float32) ** 2, axis=1)
    blocks = POINTS // PTS_DEV
    point_blocks = points.reshape(blocks, PTS_DEV, D)
    target_blocks = targets.reshape(blocks, PTS_DEV, OUTS)

    def step(grad_sum, items):
        block_points, block_targets = items
        point_norm = jnp.sum(block_points.astype(jnp.float32) ** 2, axis=1)
        inner = jnp.dot(block_points, centers.T, preferred_element_type=jnp.float32)
        distance = point_norm[:, None] + center_norm[None, :] - 2.0 * inner
        kernel = jnp.exp(-distance / D).astype(jnp.bfloat16)
        prediction = jnp.dot(kernel, coefs, preferred_element_type=jnp.float32)
        block_residual = prediction - block_targets.astype(jnp.float32)
        residual_b = block_residual.astype(jnp.bfloat16)
        grad_sum = grad_sum + jnp.dot(kernel.T, residual_b, preferred_element_type=jnp.float32)
        return grad_sum, block_residual

    grad_init = jnp.zeros((CENTERS, OUTS), jnp.float32)
    coef_grad, residual = lax.scan(step, grad_init, (point_blocks, target_blocks))
    return residual.reshape(POINTS, OUTS), coef_grad
```

```python
import functools

import jax
import jax.numpy as jnp
from jax import lax
from jax.experimental import pallas as pl
from jax.experimental.pallas import tpu as pltpu
from jax.sharding import PartitionSpec as P

F32, BF16 = jnp.float32, jnp.bfloat16
VMEM = pl.BlockSpec(memory_space=pltpu.VMEM)
ANY = pl.BlockSpec(memory_space=pl.ANY)


def dot(a, b, contract):
    return lax.dot_general(a, b, (contract, ((), ())), preferred_element_type=F32)


def piece_kernel(rows_ref, pool_ref, coefs_ref, piece_ref):
    count, width = pool_ref.shape
    picked = lax.broadcasted_iota(jnp.int32, (count, rows_ref.shape[1]), 0) == rows_ref[...]
    piece_ref[:, :width] = dot(picked.astype(F32).astype(BF16), pool_ref[...], ((0,), (0,))).astype(BF16)
    piece_ref[:, width:] = coefs_ref[...]


def points_kernel(rows_ref, pool_ref, points_ref, norm_ref, picks, squares):
    count, width = pool_ref.shape
    lane = lax.broadcasted_iota(jnp.int32, (128, 128), 1)
    for j in range(rows_ref.shape[0]):
        row = jnp.broadcast_to(rows_ref[j : j + 1, :], (128, 128)).T
        for g in range(count // 128):
            picks[j * 128 : (j + 1) * 128, g * 128 : (g + 1) * 128] = (
                (row == lane + g * 128).astype(F32).astype(BF16)
            )
    for n in range(width // 256):
        block = dot(picks[...], pool_ref[:, n * 256 : (n + 1) * 256], ((1,), (0,)))
        points_ref[:, n * 256 : (n + 1) * 256] = block.astype(BF16)
        square = block[:, :128] * block[:, :128] + block[:, 128:] * block[:, 128:]
        squares[...] = square if n == 0 else squares[...] + square
    norm_ref[...] = jnp.sum(squares[...], axis=1, keepdims=True)


def residual_kernel(pieces, width, points_ref, norm_ref, targets_ref, *refs):
    piece_refs, (residual_hbm, kept_ref, sent_ref), (centers, coefs, residual, sem) = (
        refs[:pieces],
        refs[pieces : pieces + 3],
        refs[pieces + 3 :],
    )
    each = piece_refs[0].shape[0]
    for i, ref in enumerate(piece_refs):
        centers[i * each : (i + 1) * each, :] = ref[:, :width]
        coefs[i * each : (i + 1) * each, :] = ref[:, width:]
    squares = jnp.zeros((pieces * each, 128), F32)
    for g in range(width // 128):
        part = centers[:, g * 128 : (g + 1) * 128].astype(F32)
        squares = squares + part * part
    center_norm = jnp.sum(squares.T, axis=0, keepdims=True)
    rows = 256
    grad = jnp.zeros((pieces * each, coefs.shape[1]), F32)
    copies = []
    for m in range(points_ref.shape[0] // rows):
        at = slice(m * rows, (m + 1) * rows)
        inner = dot(points_ref[at, :], centers[...], ((1,), (1,)))
        distance = norm_ref[at, :] + center_norm - 2.0 * inner
        kernel = jnp.exp(distance * (-1.0 / width)).astype(BF16)
        left = dot(kernel, coefs[...], ((1,), (0,))) - targets_ref[at, :].astype(F32)
        residual[at, :] = left
        copy = pltpu.make_async_copy(residual.at[at, :], residual_hbm.at[at, :], sem.at[m])
        copy.start()
        copies.append(copy)
        grad = grad + dot(kernel, left.astype(BF16), ((0,), (0,)))
    half = pieces * each // 2
    kept_ref[...] = grad[:half]
    sent_ref[...] = grad[half:]
    for copy in copies:
        copy.wait()


def swap(x, axes, sizes, flips):
    blk, rep = sizes
    pairs = [
        (b * rep + r, (b ^ flips[0]) * rep + (r ^ flips[1])) for b in range(blk) for r in range(rep)
    ]
    return lax.ppermute(x, axes, pairs)


def digits(size, low):
    groups = []
    while 1 << low < size:
        high = min(low + 2, size.bit_length() - 1)
        groups.append([d << low for d in range(1, 1 << (high - low))])
        low = high
    return groups


def pair_sum(parts):
    while len(parts) > 1:
        parts = [parts[i] + parts[i + 1] for i in range(0, len(parts), 2)]
    return parts[0]


def per_device(sizes, point_pool, batch_rows, targets, center_pool, center_rows, coefs):
    send = functools.partial(swap, axes=("blk", "rep"), sizes=sizes)
    each, outs = coefs.shape
    width = point_pool.shape[1]
    count = batch_rows.shape[0]

    piece = pl.pallas_call(
        piece_kernel,
        out_shape=jax.ShapeDtypeStruct((each, width + outs), BF16),
        in_specs=[VMEM] * 3,
        out_specs=VMEM,
        name="piece",
    )(center_rows.reshape(1, each), center_pool, coefs)

    chips, reps = digits(sizes[0], 1), digits(sizes[1], 0)
    held = {0: piece}
    for group in chips:
        for s, x in list(held.items()):
            for d in reversed(group):
                held[s ^ d] = send(x, flips=(d, 0))
    for s, x in list(held.items()):
        held[s ^ 1] = send(x, flips=(1, 0))

    points, point_norm = pl.pallas_call(
        points_kernel,
        out_shape=(
            jax.ShapeDtypeStruct((count, width), BF16),
            jax.ShapeDtypeStruct((count, 1), F32),
        ),
        in_specs=[VMEM] * 2,
        out_specs=(VMEM, VMEM),
        scratch_shapes=[
            pltpu.VMEM((count, point_pool.shape[0]), BF16),
            pltpu.VMEM((count, 128), F32),
        ],
        compiler_params=pltpu.CompilerParams(vmem_limit_bytes=32 << 20),
        cost_estimate=pl.CostEstimate(flops=2 << 30, bytes_accessed=5 << 20, transcendentals=0),
        name="points",
    )(batch_rows.reshape(count // 128, 128), point_pool)

    near = [0] + [d for d in chips[0]]
    far = [0]
    for group in chips[1:]:
        far = [f ^ d for d in [0] + group for f in far]
    kept_slots = [f ^ (n if n else 1) for f in far for n in near]
    slots = kept_slots + [s ^ 1 for s in kept_slots]
    residual, kept, sent = pl.pallas_call(
        functools.partial(residual_kernel, len(slots), width),
        out_shape=(
            jax.ShapeDtypeStruct((count, outs), F32),
            jax.ShapeDtypeStruct((len(kept_slots) * each, outs), F32),
            jax.ShapeDtypeStruct((len(kept_slots) * each, outs), F32),
        ),
        in_specs=[VMEM] * (3 + len(slots)),
        out_specs=(ANY, VMEM, VMEM),
        scratch_shapes=[
            pltpu.VMEM((len(slots) * each, width), BF16),
            pltpu.VMEM((len(slots) * each, outs), BF16),
            pltpu.VMEM((count, outs), F32),
            pltpu.SemaphoreType.DMA((count // 256,)),
        ],
        compiler_params=pltpu.CompilerParams(vmem_limit_bytes=32 << 20),
        name="residual",
    )(points, point_norm, targets, *[held[s] for s in slots])

    total = (kept + send(sent, flips=(1, 0))).reshape(len(far), len(near), each, outs)
    blocks = {f: total[i] for i, f in enumerate(far)}
    for group in reversed(chips[1:]):
        low = [f for f in blocks if f < group[0]]
        got = {d: {f: send(blocks[f ^ d], flips=(d, 0)) for f in low} for d in reversed(group)}
        blocks = {f: pair_sum([blocks[f]] + [got[d][f] for d in group]) for f in low}
    rows = blocks[0]
    got = {d: send(rows[i + 1], flips=(d ^ 1, 0)) for i, d in reversed(list(enumerate(chips[0])))}
    mine = pair_sum([rows[0]] + [got[d] for d in chips[0]])
    flip = 1
    for group in reps:
        got = {d: send(mine, flips=(flip, d)) for d in reversed(group)}
        first = send(mine, flips=(1, 0)) if flip else mine
        mine, flip = pair_sum([first] + [got[d] for d in group]), 0
    return residual, mine


def solution(mesh):
    return jax.shard_map(
        functools.partial(per_device, (mesh.shape["blk"], mesh.shape["rep"])),
        mesh=mesh,
        in_specs=(
            P(("blk", "rep"), None),
            P(("blk", "rep")),
            P(("blk", "rep"), None),
            P("blk", None),
            P("blk"),
            P("blk", None),
        ),
        out_specs=(P(("blk", "rep"), None), P("blk", None)),
        check_vma=False,
    )
```

```python
import functools

import jax
import jax.numpy as jnp
from jax import lax
from jax.experimental import pallas as pl
from jax.experimental.pallas import tpu as pltpu
from jax.sharding import PartitionSpec as P

F32, BF16 = jnp.float32, jnp.bfloat16
STEPS = 2
VMEM = pl.BlockSpec(memory_space=pltpu.VMEM)
ANY = pl.BlockSpec(memory_space=pl.ANY)


def in_hbm(x):
    return pltpu.with_memory_space_constraint(x, pltpu.HBM)


def dot(a, b, contract):
    return lax.dot_general(a, b, (contract, ((), ())), preferred_element_type=F32)


def start_copies(source, target, sem, parts):
    step = source.shape[0] // parts
    copies = []
    for p in range(parts):
        at = slice(p * step, (p + 1) * step)
        copies.append(pltpu.make_async_copy(source.at[at, :], target.at[at, :], sem.at[p]))
        copies[-1].start()
    return copies


def piece_kernel(rows_hbm, centers_hbm, coefs_hbm, picks_hbm, pool_hbm, piece_ref, picks_ref, pool_ref, rows_ref, centers_ref, sem, pool_sem):
    candidates, width = centers_ref.shape
    copies = [
        pltpu.make_async_copy(rows_hbm, rows_ref, sem.at[0]),
        pltpu.make_async_copy(centers_hbm, centers_ref, sem.at[1]),
        pltpu.make_async_copy(coefs_hbm, piece_ref.at[:, width:], sem.at[2]),
        pltpu.make_async_copy(picks_hbm, picks_ref, sem.at[3]),
    ]
    for copy in copies:
        copy.start()
    first = pool_ref.shape[0]
    copies += start_copies(pool_hbm.at[:first, :], pool_ref, pool_sem, pool_sem.shape[0])
    copies[0].wait()
    picked = lax.broadcasted_iota(jnp.int32, (candidates, rows_ref.shape[1]), 0) == rows_ref[...]
    picked = picked.astype(F32).astype(BF16)
    copies[1].wait()
    piece_ref[:, :width] = dot(picked, centers_ref[...], ((0,), (0,))).astype(BF16)
    for copy in copies[2:]:
        copy.wait()


def points_kernel(rows_ref, first_ref, pool_hbm, targets_hbm, points_ref, norm_ref, targets_ref, rest_ref, picks, partial, squares, sem):
    first, width = first_ref.shape
    count = first + rest_ref.shape[0]
    parts = sem.shape[0] // 2
    copies = start_copies(pool_hbm.at[first:, :], rest_ref, sem, parts)
    later = start_copies(targets_hbm, targets_ref, sem.at[parts:], parts)
    lane = lax.broadcasted_iota(jnp.int32, (128, 128), 1).astype(jnp.int16)
    one, zero = jnp.ones((128, 128), BF16), jnp.zeros((128, 128), BF16)
    for j in range(rows_ref.shape[0]):
        row = jnp.broadcast_to(rows_ref[j : j + 1, :], (128, 128)).T.astype(jnp.int16)
        for g in range(count // 128):
            picks[j * 128 : (j + 1) * 128, g * 128 : (g + 1) * 128] = (
                jnp.where(row == lane + jnp.int16(g * 128), one, zero)
            )
    for n in range(width // 256):
        at = slice(n * 256, (n + 1) * 256)
        partial[:, at] = dot(picks[:, :first], first_ref[:, at], ((1,), (0,)))
    for copy in copies:
        copy.wait()
    for n in range(width // 256):
        at = slice(n * 256, (n + 1) * 256)
        block = partial[:, at] + dot(picks[:, first:], rest_ref[:, at], ((1,), (0,)))
        points_ref[:, at] = block.astype(BF16)
        square = block[:, :128] * block[:, :128] + block[:, 128:] * block[:, 128:]
        squares[...] = square if n == 0 else squares[...] + square
    norm_ref[...] = jnp.sum(squares[...], axis=1, keepdims=True)
    for copy in later:
        copy.wait()


def residual_kernel(far, each, points_ref, norm_ref, targets_ref, own_ref, other_ref, residual_hbm, kept_ref, sent_ref, centers, coefs, kernel, rounded, residual, sem):
    half = own_ref.shape[0]
    count, width = points_ref.shape
    for i, ref in enumerate((own_ref, other_ref)):
        centers[i * half : (i + 1) * half, :] = ref[:, :width]
        coefs[i * half : (i + 1) * half, :] = ref[:, width:]
    squares = jnp.zeros((2 * half, 128), F32)
    for g in range(width // 128):
        part = centers[:, g * 128 : (g + 1) * 128].astype(F32)
        squares = squares + part * part
    center_norm = jnp.sum(squares.T, axis=0, keepdims=True)
    rows = count // STEPS
    copies = []
    for m in range(STEPS):
        at = slice(m * rows, (m + 1) * rows)
        inner = dot(points_ref[at, :], centers[...], ((1,), (1,)))
        distance = norm_ref[at, :] + center_norm - 2.0 * inner
        kernel[at, :] = jnp.exp(distance * (-1.0 / width)).astype(BF16)
    for m in range(STEPS):
        at = slice(m * rows, (m + 1) * rows)
        left = dot(kernel[at, :], coefs[...], ((1,), (0,))) - targets_ref[at, :].astype(F32)
        residual[at, :] = left
        rounded[at, :] = left.astype(BF16)
        copies.append(pltpu.make_async_copy(residual.at[at, :], residual_hbm.at[at, :], sem.at[m]))
        copies[-1].start()
    grad = dot(kernel[...], rounded[...], ((0,), (0,)))
    step = half // far
    for f in range(far):
        at = f * step
        kept_ref[at : at + each, :] = grad[half + at : half + at + each]
        kept_ref[at + each : at + step, :] = grad[at + each : at + step]
        sent_ref[at : at + each, :] = grad[at : at + each]
        sent_ref[at + each : at + step, :] = grad[half + at + each : half + at + step]
    for copy in copies:
        copy.wait()


def swap(x, axes, sizes, flips):
    blk, rep = sizes
    pairs = [
        (b * rep + r, (b ^ flips[0]) * rep + (r ^ flips[1])) for b in range(blk) for r in range(rep)
    ]
    return lax.ppermute(x, axes, pairs)


def digits(size, low):
    groups = []
    while 1 << low < size:
        high = min(low + 2, size.bit_length() - 1)
        groups.append([d << low for d in range(1, 1 << (high - low))])
        low = high
    return groups


def pair_sum(parts):
    while len(parts) > 1:
        parts = [parts[i] + parts[i + 1] for i in range(0, len(parts), 2)]
    return parts[0]


def per_device(sizes, point_pool, batch_rows, targets, center_pool, center_rows, coefs):
    send = functools.partial(swap, axes=("blk", "rep"), sizes=sizes)
    each, outs = coefs.shape
    width = point_pool.shape[1]
    count = batch_rows.shape[0]

    rows = batch_rows.reshape(count // 128, 128)
    pool = in_hbm(point_pool)
    first = point_pool.shape[0] // 512 * 256
    piece, rows, resident = pl.pallas_call(
        piece_kernel,
        out_shape=(
            pltpu.VMEM((each, width + outs), BF16),
            pltpu.VMEM(rows.shape, rows.dtype),
            pltpu.VMEM((first, width), BF16),
        ),
        in_specs=[ANY] * 5,
        out_specs=(VMEM,) * 3,
        scratch_shapes=[
            pltpu.VMEM((1, each), jnp.int32),
            pltpu.VMEM(center_pool.shape, BF16),
            pltpu.SemaphoreType.DMA((4,)),
            pltpu.SemaphoreType.DMA((4,)),
        ],
        compiler_params=pltpu.CompilerParams(vmem_limit_bytes=8 << 20),
        name="piece",
    )(in_hbm(center_rows.reshape(1, each)), in_hbm(center_pool), in_hbm(coefs), in_hbm(rows), pool)

    chips, reps = digits(sizes[0], 1), digits(sizes[1], 0)
    block = piece
    parts = [block] + [send(block, flips=(d, 0)) for d in chips[0]]
    points, point_norm, goals = pl.pallas_call(
        points_kernel,
        out_shape=(
            pltpu.VMEM((count, width), BF16),
            pltpu.VMEM((count, 1), F32),
            pltpu.VMEM(targets.shape, BF16),
        ),
        in_specs=[VMEM, VMEM, ANY, ANY],
        out_specs=(VMEM,) * 3,
        scratch_shapes=[
            pltpu.VMEM((point_pool.shape[0] - first, width), BF16),
            pltpu.VMEM((count, point_pool.shape[0]), BF16),
            pltpu.VMEM((count, width), F32),
            pltpu.VMEM((count, 128), F32),
            pltpu.SemaphoreType.DMA((8,)),
        ],
        compiler_params=pltpu.CompilerParams(vmem_limit_bytes=32 << 20),
        cost_estimate=pl.CostEstimate(flops=2 << 30, bytes_accessed=5 << 20, transcendentals=0),
        name="points",
    )(rows, resident, pool, in_hbm(targets))
    parts, points, point_norm, goals = lax.optimization_barrier((parts, points, point_norm, goals))
    block = jnp.concatenate(parts, axis=0)
    near = len(parts)
    for group in chips[1:]:
        block = jnp.concatenate([block] + [send(block, flips=(d, 0)) for d in group], axis=0)
    half = block.shape[0]
    far = half // (near * each)
    residual, kept, sent = pl.pallas_call(
        functools.partial(residual_kernel, far, each),
        out_shape=(
            jax.ShapeDtypeStruct((count, outs), F32),
            pltpu.VMEM((half, outs), F32),
            pltpu.VMEM((half, outs), F32),
        ),
        in_specs=[VMEM] * 5,
        out_specs=(ANY, VMEM, VMEM),
        scratch_shapes=[
            pltpu.VMEM((2 * half, width), BF16),
            pltpu.VMEM((2 * half, outs), BF16),
            pltpu.VMEM((count, 2 * half), BF16),
            pltpu.VMEM((count, outs), BF16),
            pltpu.VMEM((count, outs), F32),
            pltpu.SemaphoreType.DMA((STEPS,)),
        ],
        compiler_params=pltpu.CompilerParams(vmem_limit_bytes=32 << 20),
        name="residual",
    )(points, point_norm, goals, block, send(block, flips=(1, 0)))

    total = (kept + send(sent, flips=(1, 0))).reshape(far, near, each, outs)
    for group in reversed(chips[1:]):
        low = total.shape[0] // (len(group) + 1)
        blocks = [total[i * low : (i + 1) * low] for i in range(len(group) + 1)]
        total = pair_sum(blocks[:1] + [send(x, flips=(d, 0)) for x, d in zip(blocks[1:], group)])
    mine = pair_sum([total[0, 0]] + [send(total[0, i + 1], flips=(d ^ 1, 0)) for i, d in enumerate(chips[0])])
    flip = 1
    for group in reps:
        first = send(mine, flips=(1, 0)) if flip else mine
        mine, flip = pair_sum([first] + [send(mine, flips=(flip, d)) for d in group]), 0
    return residual, mine


def solution(mesh):
    return jax.shard_map(
        functools.partial(per_device, (mesh.shape["blk"], mesh.shape["rep"])),
        mesh=mesh,
        in_specs=(
            P(("blk", "rep"), None),
            P(("blk", "rep")),
            P(("blk", "rep"), None),
            P("blk", None),
            P("blk"),
            P("blk", None),
        ),
        out_specs=(P(("blk", "rep"), None), P("blk", None)),
        check_vma=False,
    )
```

```python
import functools

import jax
import jax.numpy as jnp
from jax import lax
from jax.experimental import pallas as pl
from jax.experimental.pallas import tpu as pltpu
from jax.sharding import PartitionSpec as P

F32, BF16 = jnp.float32, jnp.bfloat16
STEPS = 2
VMEM = pl.BlockSpec(memory_space=pltpu.VMEM)
ANY = pl.BlockSpec(memory_space=pl.ANY)


def in_hbm(x):
    return pltpu.with_memory_space_constraint(x, pltpu.HBM)


def dot(a, b, contract):
    return lax.dot_general(a, b, (contract, ((), ())), preferred_element_type=F32)


def start_copies(source, target, sem, parts):
    step = source.shape[0] // parts
    copies = []
    for p in range(parts):
        at = slice(p * step, (p + 1) * step)
        copies.append(pltpu.make_async_copy(source.at[at, :], target.at[at, :], sem.at[p]))
        copies[-1].start()
    return copies


def piece_kernel(rows_hbm, centers_hbm, coefs_hbm, picks_hbm, pool_hbm, piece_ref, picks_ref, pool_ref, rows_ref, centers_ref, sem, pool_sem):
    candidates, width = centers_ref.shape
    copies = [
        pltpu.make_async_copy(rows_hbm, rows_ref, sem.at[0]),
        pltpu.make_async_copy(centers_hbm, centers_ref, sem.at[1]),
        pltpu.make_async_copy(coefs_hbm, piece_ref.at[:, width:], sem.at[2]),
        pltpu.make_async_copy(picks_hbm, picks_ref, sem.at[3]),
    ]
    for copy in copies:
        copy.start()
    first = pool_ref.shape[0]
    copies += start_copies(pool_hbm.at[:first, :], pool_ref, pool_sem, pool_sem.shape[0])
    copies[0].wait()
    picked = lax.broadcasted_iota(jnp.int32, (candidates, rows_ref.shape[1]), 0) == rows_ref[...]
    picked = picked.astype(F32).astype(BF16)
    copies[1].wait()
    piece_ref[:, :width] = dot(picked, centers_ref[...], ((0,), (0,))).astype(BF16)
    for copy in copies[2:]:
        copy.wait()


def points_kernel(rows_ref, first_ref, pool_hbm, targets_hbm, points_ref, norm_ref, targets_ref, rest_ref, picks, partial, squares, sem):
    first, width = first_ref.shape
    count = first + rest_ref.shape[0]
    parts = sem.shape[0] // 2
    copies = start_copies(pool_hbm.at[first:, :], rest_ref, sem, parts)
    later = start_copies(targets_hbm, targets_ref, sem.at[parts:], parts)
    lane = lax.broadcasted_iota(jnp.int32, (128, 128), 1).astype(jnp.int16)
    one, zero = jnp.ones((128, 128), BF16), jnp.zeros((128, 128), BF16)
    for j in range(rows_ref.shape[0]):
        row = jnp.broadcast_to(rows_ref[j : j + 1, :], (128, 128)).T.astype(jnp.int16)
        for g in range(count // 128):
            picks[j * 128 : (j + 1) * 128, g * 128 : (g + 1) * 128] = (
                jnp.where(row == lane + jnp.int16(g * 128), one, zero)
            )
    for n in range(width // 256):
        at = slice(n * 256, (n + 1) * 256)
        partial[:, at] = dot(picks[:, :first], first_ref[:, at], ((1,), (0,)))
    for copy in copies:
        copy.wait()
    for n in range(width // 256):
        at = slice(n * 256, (n + 1) * 256)
        block = partial[:, at] + dot(picks[:, first:], rest_ref[:, at], ((1,), (0,)))
        points_ref[:, at] = block.astype(BF16)
        square = block[:, :128] * block[:, :128] + block[:, 128:] * block[:, 128:]
        squares[...] = square if n == 0 else squares[...] + square
    norm_ref[...] = jnp.sum(squares[...], axis=1, keepdims=True)
    for copy in later:
        copy.wait()


def residual_kernel(far, each, points_ref, norm_ref, targets_ref, own_ref, other_ref, residual_ref, kept_ref, sent_ref, centers, coefs, kernel, rounded):
    half = own_ref.shape[0]
    count, width = points_ref.shape
    for i, ref in enumerate((own_ref, other_ref)):
        centers[i * half : (i + 1) * half, :] = ref[:, :width]
        coefs[i * half : (i + 1) * half, :] = ref[:, width:]
    squares = jnp.zeros((2 * half, 128), F32)
    for g in range(width // 128):
        part = centers[:, g * 128 : (g + 1) * 128].astype(F32)
        squares = squares + part * part
    center_norm = jnp.sum(squares.T, axis=0, keepdims=True)
    rows = count // STEPS
    for m in range(STEPS):
        at = slice(m * rows, (m + 1) * rows)
        inner = dot(points_ref[at, :], centers[...], ((1,), (1,)))
        distance = norm_ref[at, :] + center_norm - 2.0 * inner
        kernel[at, :] = jnp.exp(distance * (-1.0 / width)).astype(BF16)
    for m in range(STEPS):
        at = slice(m * rows, (m + 1) * rows)
        left = dot(kernel[at, :], coefs[...], ((1,), (0,))) - targets_ref[at, :].astype(F32)
        residual_ref[at, :] = left
        rounded[at, :] = left.astype(BF16)
    grad = dot(kernel[...], rounded[...], ((0,), (0,)))
    step = half // far
    for f in range(far):
        at = f * step
        kept_ref[at : at + each, :] = grad[half + at : half + at + each]
        kept_ref[at + each : at + step, :] = grad[at + each : at + step]
        sent_ref[at : at + each, :] = grad[at : at + each]
        sent_ref[at + each : at + step, :] = grad[half + at + each : half + at + step]


def write_kernel(source, target, sem):
    for copy in start_copies(source, target, sem, sem.shape[0]):
        copy.wait()


def swap(x, axes, sizes, flips):
    blk, rep = sizes
    pairs = [
        (b * rep + r, (b ^ flips[0]) * rep + (r ^ flips[1])) for b in range(blk) for r in range(rep)
    ]
    return lax.ppermute(x, axes, pairs)


def digits(size, low):
    groups = []
    while 1 << low < size:
        high = min(low + 2, size.bit_length() - 1)
        groups.append([d << low for d in range(1, 1 << (high - low))])
        low = high
    return groups


def pair_sum(parts):
    while len(parts) > 1:
        parts = [parts[i] + parts[i + 1] for i in range(0, len(parts), 2)]
    return parts[0]


def per_device(sizes, point_pool, batch_rows, targets, center_pool, center_rows, coefs):
    send = functools.partial(swap, axes=("blk", "rep"), sizes=sizes)
    each, outs = coefs.shape
    width = point_pool.shape[1]
    count = batch_rows.shape[0]

    rows = batch_rows.reshape(count // 128, 128)
    pool = in_hbm(point_pool)
    first = point_pool.shape[0] // 512 * 256
    piece, rows, resident = pl.pallas_call(
        piece_kernel,
        out_shape=(
            pltpu.VMEM((each, width + outs), BF16),
            pltpu.VMEM(rows.shape, rows.dtype),
            pltpu.VMEM((first, width), BF16),
        ),
        in_specs=[ANY] * 5,
        out_specs=(VMEM,) * 3,
        scratch_shapes=[
            pltpu.VMEM((1, each), jnp.int32),
            pltpu.VMEM(center_pool.shape, BF16),
            pltpu.SemaphoreType.DMA((4,)),
            pltpu.SemaphoreType.DMA((4,)),
        ],
        compiler_params=pltpu.CompilerParams(vmem_limit_bytes=8 << 20),
        name="piece",
    )(in_hbm(center_rows.reshape(1, each)), in_hbm(center_pool), in_hbm(coefs), in_hbm(rows), pool)

    chips, reps = digits(sizes[0], 1), digits(sizes[1], 0)
    block = piece
    near = [0] + chips[0]
    parts = [block] + [send(block, flips=(d, 0)) for d in near[1:]]
    points, point_norm, goals = pl.pallas_call(
        points_kernel,
        out_shape=(
            pltpu.VMEM((count, width), BF16),
            pltpu.VMEM((count, 1), F32),
            pltpu.VMEM(targets.shape, BF16),
        ),
        in_specs=[VMEM, VMEM, ANY, ANY],
        out_specs=(VMEM,) * 3,
        scratch_shapes=[
            pltpu.VMEM((point_pool.shape[0] - first, width), BF16),
            pltpu.VMEM((count, point_pool.shape[0]), BF16),
            pltpu.VMEM((count, width), F32),
            pltpu.VMEM((count, 128), F32),
            pltpu.SemaphoreType.DMA((8,)),
        ],
        compiler_params=pltpu.CompilerParams(vmem_limit_bytes=32 << 20),
        cost_estimate=pl.CostEstimate(flops=2 << 30, bytes_accessed=5 << 20, transcendentals=0),
        name="points",
    )(rows, resident, pool, in_hbm(targets))
    parts, points, point_norm, goals = lax.optimization_barrier((parts, points, point_norm, goals))
    block = jnp.concatenate(parts, axis=0)
    for group in chips[1:]:
        block = jnp.concatenate([block] + [send(block, flips=(d, 0)) for d in group], axis=0)
    half = block.shape[0]
    far = half // (len(near) * each)
    residual, kept, sent = pl.pallas_call(
        functools.partial(residual_kernel, far, each),
        out_shape=(
            pltpu.VMEM((count, outs), F32),
            pltpu.VMEM((half, outs), F32),
            pltpu.VMEM((half, outs), F32),
        ),
        in_specs=[VMEM] * 5,
        out_specs=(VMEM,) * 3,
        scratch_shapes=[
            pltpu.VMEM((2 * half, width), BF16),
            pltpu.VMEM((2 * half, outs), BF16),
            pltpu.VMEM((count, 2 * half), BF16),
            pltpu.VMEM((count, outs), BF16),
        ],
        compiler_params=pltpu.CompilerParams(vmem_limit_bytes=32 << 20),
        name="residual",
    )(points, point_norm, goals, block, send(block, flips=(1, 0)))

    total = (kept + send(sent, flips=(1, 0))).reshape(far, len(near), each, outs)
    for group in reversed(chips[1:]):
        low = total.shape[0] // (len(group) + 1)
        blocks = [total[i * low : (i + 1) * low] for i in range(len(group) + 1)]
        total = pair_sum(blocks[:1] + [send(x, flips=(d, 0)) for x, d in zip(blocks[1:], group)])
    rows = {d: total[0, i] for i, d in enumerate(near)}
    parts = [rows[0]] + [send(rows[d], flips=(d ^ 1, 0)) for d in chips[0]]
    residual = pl.pallas_call(
        write_kernel,
        out_shape=jax.ShapeDtypeStruct(residual.shape, F32),
        in_specs=[VMEM],
        out_specs=ANY,
        scratch_shapes=[pltpu.SemaphoreType.DMA((4,))],
        compiler_params=pltpu.CompilerParams(vmem_limit_bytes=8 << 20),
        cost_estimate=pl.CostEstimate(flops=0, bytes_accessed=4 << 20, transcendentals=0),
        name="write",
    )(residual)
    parts, residual = lax.optimization_barrier((parts, residual))
    mine = pair_sum(parts)
    flip = 1
    for group in reps:
        first = send(mine, flips=(1, 0)) if flip else mine
        mine, flip = pair_sum([first] + [send(mine, flips=(flip, d)) for d in group]), 0
    return residual, mine


def solution(mesh):
    return jax.shard_map(
        functools.partial(per_device, (mesh.shape["blk"], mesh.shape["rep"])),
        mesh=mesh,
        in_specs=(
            P(("blk", "rep"), None),
            P(("blk", "rep")),
            P(("blk", "rep"), None),
            P("blk", None),
            P("blk"),
            P("blk", None),
        ),
        out_specs=(P(("blk", "rep"), None), P("blk", None)),
        check_vma=False,
    )
```

```python
import functools

import jax
import jax.numpy as jnp
from jax import lax
from jax.experimental import pallas as pl
from jax.experimental.pallas import tpu as pltpu
from jax.sharding import PartitionSpec as P

F32, BF16 = jnp.float32, jnp.bfloat16
STEPS = 2
VMEM = pl.BlockSpec(memory_space=pltpu.VMEM)
ANY = pl.BlockSpec(memory_space=pl.ANY)


def in_hbm(x):
    return pltpu.with_memory_space_constraint(x, pltpu.HBM)


def dot(a, b, contract):
    return lax.dot_general(a, b, (contract, ((), ())), preferred_element_type=F32)


def start_copies(source, target, sem, parts):
    step = source.shape[0] // parts
    copies = []
    for p in range(parts):
        at = slice(p * step, (p + 1) * step)
        copies.append(pltpu.make_async_copy(source.at[at, :], target.at[at, :], sem.at[p]))
        copies[-1].start()
    return copies


def piece_kernel(rows_hbm, centers_hbm, coefs_hbm, picks_hbm, pool_hbm, piece_ref, picks_ref, pool_ref, rows_ref, centers_ref, sem, pool_sem):
    candidates, width = centers_ref.shape
    copies = [
        pltpu.make_async_copy(rows_hbm, rows_ref, sem.at[0]),
        pltpu.make_async_copy(centers_hbm, centers_ref, sem.at[1]),
        pltpu.make_async_copy(coefs_hbm, piece_ref.at[:, width:], sem.at[2]),
        pltpu.make_async_copy(picks_hbm, picks_ref, sem.at[3]),
    ]
    for copy in copies:
        copy.start()
    first = pool_ref.shape[0]
    copies += start_copies(pool_hbm.at[:first, :], pool_ref, pool_sem, pool_sem.shape[0])
    copies[0].wait()
    picked = lax.broadcasted_iota(jnp.int32, (candidates, rows_ref.shape[1]), 0) == rows_ref[...]
    picked = picked.astype(F32).astype(BF16)
    copies[1].wait()
    piece_ref[:, :width] = dot(picked, centers_ref[...], ((0,), (0,))).astype(BF16)
    for copy in copies[2:]:
        copy.wait()


def points_kernel(rows_ref, first_ref, pool_hbm, targets_hbm, points_ref, norm_ref, targets_ref, rest_ref, picks, partial, squares, sem):
    first, width = first_ref.shape
    count = first + rest_ref.shape[0]
    parts = sem.shape[0] // 2
    copies = start_copies(pool_hbm.at[first:, :], rest_ref, sem, parts)
    later = start_copies(targets_hbm, targets_ref, sem.at[parts:], parts)
    lane = lax.broadcasted_iota(jnp.int32, (128, 128), 1).astype(jnp.int16)
    one, zero = jnp.ones((128, 128), BF16), jnp.zeros((128, 128), BF16)
    for j in range(rows_ref.shape[0]):
        row = jnp.broadcast_to(rows_ref[j : j + 1, :], (128, 128)).T.astype(jnp.int16)
        for g in range(count // 128):
            picks[j * 128 : (j + 1) * 128, g * 128 : (g + 1) * 128] = (
                jnp.where(row == lane + jnp.int16(g * 128), one, zero)
            )
    for n in range(width // 256):
        at = slice(n * 256, (n + 1) * 256)
        partial[:, at] = dot(picks[:, :first], first_ref[:, at], ((1,), (0,)))
    for copy in copies:
        copy.wait()
    for n in range(width // 256):
        at = slice(n * 256, (n + 1) * 256)
        block = partial[:, at] + dot(picks[:, first:], rest_ref[:, at], ((1,), (0,)))
        points_ref[:, at] = block.astype(BF16)
        square = block[:, :128] * block[:, :128] + block[:, 128:] * block[:, 128:]
        squares[...] = square if n == 0 else squares[...] + square
    norm_ref[...] = jnp.sum(squares[...], axis=1, keepdims=True)
    for copy in later:
        copy.wait()


def residual_kernel(far, each, points_ref, norm_ref, targets_ref, own_ref, other_ref, residual_ref, kept_ref, sent_ref, centers, coefs, kernel, rounded):
    half = own_ref.shape[0]
    count, width = points_ref.shape
    for i, ref in enumerate((own_ref, other_ref)):
        centers[i * half : (i + 1) * half, :] = ref[:, :width]
        coefs[i * half : (i + 1) * half, :] = ref[:, width:]
    squares = jnp.zeros((2 * half, 128), F32)
    for g in range(width // 128):
        part = centers[:, g * 128 : (g + 1) * 128].astype(F32)
        squares = squares + part * part
    center_norm = jnp.sum(squares.T, axis=0, keepdims=True)
    rows = count // STEPS
    for m in range(STEPS):
        at = slice(m * rows, (m + 1) * rows)
        inner = dot(points_ref[at, :], centers[...], ((1,), (1,)))
        distance = norm_ref[at, :] + center_norm - 2.0 * inner
        kernel[at, :] = jnp.exp(distance * (-1.0 / width)).astype(BF16)
    for m in range(STEPS):
        at = slice(m * rows, (m + 1) * rows)
        left = dot(kernel[at, :], coefs[...], ((1,), (0,))) - targets_ref[at, :].astype(F32)
        residual_ref[at, :] = left
        rounded[at, :] = left.astype(BF16)
    grad = dot(kernel[...], rounded[...], ((0,), (0,)))
    step = half // far
    for f in range(far):
        at = f * step
        kept_ref[at : at + each, :] = grad[half + at : half + at + each]
        kept_ref[at + each : at + step, :] = grad[at + each : at + step]
        sent_ref[at : at + each, :] = grad[at : at + each]
        sent_ref[at + each : at + step, :] = grad[half + at + each : half + at + step]


def write_kernel(source, target, sem):
    for copy in start_copies(source, target, sem, sem.shape[0]):
        copy.wait()


def sum_kernel(*refs):
    *parts, total_ref = [ref[...] for ref in refs[:-1]] + [refs[-1]]
    parts = parts[:1] + parts[:0:-1]
    while len(parts) > 1:
        parts = [a + b for a, b in zip(parts[: len(parts) // 2], parts[len(parts) // 2 :])]
    total_ref[...] = parts[0]


def send(x, sizes, flip, shift=0, step=1, size=1):
    blk, rep = sizes
    pairs = []
    for b in range(blk):
        for r in range(rep):
            digit = r // step % size
            pairs.append((b * rep + r, (b ^ flip) * rep + r + ((digit + shift) % size - digit) * step))
    return lax.ppermute(x, ("blk", "rep"), pairs)


def digits(size, low):
    end = size.bit_length() - 1
    return [(bit, min(bit + 2, end)) for bit in range(low, end, 2)]


def pair_sum(parts):
    while len(parts) > 1:
        parts = [parts[i] + parts[i + 1] for i in range(0, len(parts), 2)]
    return parts[0]


def per_device(sizes, point_pool, batch_rows, targets, center_pool, center_rows, coefs):
    to = functools.partial(send, sizes=sizes)
    each, outs = coefs.shape
    width = point_pool.shape[1]
    count = batch_rows.shape[0]

    rows = batch_rows.reshape(count // 128, 128)
    pool = in_hbm(point_pool)
    first = point_pool.shape[0] // 512 * 256
    piece, rows, resident = pl.pallas_call(
        piece_kernel,
        out_shape=(
            pltpu.VMEM((each, width + outs), BF16),
            pltpu.VMEM(rows.shape, rows.dtype),
            pltpu.VMEM((first, width), BF16),
        ),
        in_specs=[ANY] * 5,
        out_specs=(VMEM,) * 3,
        scratch_shapes=[
            pltpu.VMEM((1, each), jnp.int32),
            pltpu.VMEM(center_pool.shape, BF16),
            pltpu.SemaphoreType.DMA((4,)),
            pltpu.SemaphoreType.DMA((4,)),
        ],
        compiler_params=pltpu.CompilerParams(vmem_limit_bytes=8 << 20),
        name="piece",
    )(in_hbm(center_rows.reshape(1, each)), in_hbm(center_pool), in_hbm(coefs), in_hbm(rows), pool)

    chips = [[d << low for d in range(1, 1 << (high - low))] for low, high in digits(sizes[0], 1)]
    reps = digits(sizes[1], 0)
    block = piece
    near = [0] + chips[0]
    parts = [block] + [to(block, flip=d) for d in near[1:]]
    points, point_norm, goals = pl.pallas_call(
        points_kernel,
        out_shape=(
            pltpu.VMEM((count, width), BF16),
            pltpu.VMEM((count, 1), F32),
            pltpu.VMEM(targets.shape, BF16),
        ),
        in_specs=[VMEM, VMEM, ANY, ANY],
        out_specs=(VMEM,) * 3,
        scratch_shapes=[
            pltpu.VMEM((point_pool.shape[0] - first, width), BF16),
            pltpu.VMEM((count, point_pool.shape[0]), BF16),
            pltpu.VMEM((count, width), F32),
            pltpu.VMEM((count, 128), F32),
            pltpu.SemaphoreType.DMA((8,)),
        ],
        compiler_params=pltpu.CompilerParams(vmem_limit_bytes=32 << 20),
        cost_estimate=pl.CostEstimate(flops=2 << 30, bytes_accessed=5 << 20, transcendentals=0),
        name="points",
    )(rows, resident, pool, in_hbm(targets))
    parts, points, point_norm, goals = lax.optimization_barrier((parts, points, point_norm, goals))
    block = jnp.concatenate(parts, axis=0)
    for group in chips[1:]:
        block = jnp.concatenate([block] + [to(block, flip=d) for d in group], axis=0)
    half = block.shape[0]
    far = half // (len(near) * each)
    residual, kept, sent = pl.pallas_call(
        functools.partial(residual_kernel, far, each),
        out_shape=(
            pltpu.VMEM((count, outs), F32),
            pltpu.VMEM((half, outs), F32),
            pltpu.VMEM((half, outs), F32),
        ),
        in_specs=[VMEM] * 5,
        out_specs=(VMEM,) * 3,
        scratch_shapes=[
            pltpu.VMEM((2 * half, width), BF16),
            pltpu.VMEM((2 * half, outs), BF16),
            pltpu.VMEM((count, 2 * half), BF16),
            pltpu.VMEM((count, outs), BF16),
        ],
        compiler_params=pltpu.CompilerParams(vmem_limit_bytes=32 << 20),
        name="residual",
    )(points, point_norm, goals, block, to(block, flip=1))

    total = (kept + to(sent, flip=1)).reshape(far, len(near), each, outs)
    for group in reversed(chips[1:]):
        low = total.shape[0] // (len(group) + 1)
        blocks = [total[i * low : (i + 1) * low] for i in range(len(group) + 1)]
        total = pair_sum(blocks[:1] + [to(x, flip=d) for x, d in zip(blocks[1:], group)])
    rows = {d: total[0, i] for i, d in enumerate(near)}
    parts = [rows[0]] + [to(rows[d], flip=d ^ 1) for d in chips[0]]
    residual = pl.pallas_call(
        write_kernel,
        out_shape=jax.ShapeDtypeStruct(residual.shape, F32),
        in_specs=[VMEM],
        out_specs=ANY,
        scratch_shapes=[pltpu.SemaphoreType.DMA((4,))],
        compiler_params=pltpu.CompilerParams(vmem_limit_bytes=8 << 20),
        cost_estimate=pl.CostEstimate(flops=0, bytes_accessed=4 << 20, transcendentals=0),
        name="write",
    )(residual)
    parts, residual = lax.optimization_barrier((parts, residual))
    mine = pair_sum(parts)
    flip = 1
    for low, high in reps:
        size = 1 << (high - low)
        around = [to(mine, flip=flip, shift=k, step=1 << low, size=size) for k in range(1, size)]
        mine = pl.pallas_call(
            sum_kernel,
            out_shape=jax.ShapeDtypeStruct(mine.shape, F32),
            in_specs=[VMEM] * size,
            out_specs=VMEM,
            compiler_params=pltpu.CompilerParams(vmem_limit_bytes=4 << 20),
            name="sum",
        )(to(mine, flip=1) if flip else mine, *around[::-1])
        flip = 0
    return residual, mine


def solution(mesh):
    return jax.shard_map(
        functools.partial(per_device, (mesh.shape["blk"], mesh.shape["rep"])),
        mesh=mesh,
        in_specs=(
            P(("blk", "rep"), None),
            P(("blk", "rep")),
            P(("blk", "rep"), None),
            P("blk", None),
            P("blk"),
            P("blk", None),
        ),
        out_specs=(P(("blk", "rep"), None), P("blk", None)),
        check_vma=False,
    )
```

```python
import functools
import math

import jax
import jax.numpy as jnp
from jax import lax
from jax.experimental import pallas as pl
from jax.experimental.pallas import tpu as pltpu
from jax.sharding import PartitionSpec as P

F32, BF16 = jnp.float32, jnp.bfloat16
STEPS = 2
ACROSS = (1, 1, 0, 0)
VMEM = pl.BlockSpec(memory_space=pltpu.VMEM)
ANY = pl.BlockSpec(memory_space=pl.ANY)


def in_hbm(x):
    return pltpu.with_memory_space_constraint(x, pltpu.HBM)


def dot(a, b, contract):
    return lax.dot_general(a, b, (contract, ((), ())), preferred_element_type=F32)


def start_copies(source, target, sem, parts):
    step = source.shape[0] // parts
    copies = []
    for p in range(parts):
        at = slice(p * step, (p + 1) * step)
        copies.append(pltpu.make_async_copy(source.at[at, :], target.at[at, :], sem.at[p]))
        copies[-1].start()
    return copies


def piece_kernel(rows_hbm, centers_hbm, coefs_hbm, picks_hbm, pool_hbm, piece_ref, picks_ref, pool_ref, rows_ref, centers_ref, sem, pool_sem):
    candidates, width = centers_ref.shape
    copies = [
        pltpu.make_async_copy(rows_hbm, rows_ref, sem.at[0]),
        pltpu.make_async_copy(centers_hbm, centers_ref, sem.at[1]),
        pltpu.make_async_copy(coefs_hbm, piece_ref.at[:, width:], sem.at[2]),
        pltpu.make_async_copy(picks_hbm, picks_ref, sem.at[3]),
    ]
    for copy in copies:
        copy.start()
    first = pool_ref.shape[0]
    copies += start_copies(pool_hbm.at[:first, :], pool_ref, pool_sem, pool_sem.shape[0])
    copies[0].wait()
    picked = lax.broadcasted_iota(jnp.int32, (candidates, rows_ref.shape[1]), 0) == rows_ref[...]
    picked = picked.astype(F32).astype(BF16)
    copies[1].wait()
    piece_ref[:, :width] = dot(picked, centers_ref[...], ((0,), (0,))).astype(BF16)
    for copy in copies[2:]:
        copy.wait()


def points_kernel(rows_ref, first_ref, pool_hbm, targets_hbm, points_ref, norm_ref, targets_ref, rest_ref, picks, partial, squares, sem):
    first, width = first_ref.shape
    count = first + rest_ref.shape[0]
    parts = sem.shape[0] // 2
    copies = start_copies(pool_hbm.at[first:, :], rest_ref, sem, parts)
    later = start_copies(targets_hbm, targets_ref, sem.at[parts:], parts)
    lane = lax.broadcasted_iota(jnp.int32, (128, 128), 1).astype(jnp.int16)
    one, zero = jnp.ones((128, 128), BF16), jnp.zeros((128, 128), BF16)
    for j in range(rows_ref.shape[0]):
        row = jnp.broadcast_to(rows_ref[j : j + 1, :], (128, 128)).T.astype(jnp.int16)
        for g in range(count // 128):
            picks[j * 128 : (j + 1) * 128, g * 128 : (g + 1) * 128] = (
                jnp.where(row == lane + jnp.int16(g * 128), one, zero)
            )
    for n in range(width // 256):
        at = slice(n * 256, (n + 1) * 256)
        partial[:, at] = dot(picks[:, :first], first_ref[:, at], ((1,), (0,)))
    for copy in copies:
        copy.wait()
    for n in range(width // 256):
        at = slice(n * 256, (n + 1) * 256)
        block = partial[:, at] + dot(picks[:, first:], rest_ref[:, at], ((1,), (0,)))
        points_ref[:, at] = block.astype(BF16)
        square = block[:, :128] * block[:, :128] + block[:, 128:] * block[:, 128:]
        squares[...] = square if n == 0 else squares[...] + square
    norm_ref[...] = jnp.sum(squares[...], axis=1, keepdims=True)
    for copy in later:
        copy.wait()


def residual_kernel(far, each, points_ref, norm_ref, targets_ref, own_ref, other_ref, residual_ref, kept_ref, sent_ref, centers, coefs, kernel, rounded):
    half = own_ref.shape[0]
    count, width = points_ref.shape
    for i, ref in enumerate((own_ref, other_ref)):
        centers[i * half : (i + 1) * half, :] = ref[:, :width]
        coefs[i * half : (i + 1) * half, :] = ref[:, width:]
    squares = jnp.zeros((2 * half, 128), F32)
    for g in range(width // 128):
        part = centers[:, g * 128 : (g + 1) * 128].astype(F32)
        squares = squares + part * part
    scale = 1.0 / (width * math.log(2.0))
    center_norm = jnp.sum(squares.T, axis=0, keepdims=True) * -scale
    rows = count // STEPS
    for m in range(STEPS):
        at = slice(m * rows, (m + 1) * rows)
        inner = dot(points_ref[at, :], centers[...], ((1,), (1,)))
        norms = norm_ref[at, :] * -scale + center_norm
        kernel[at, :] = jnp.exp2(norms + inner * (2.0 * scale)).astype(BF16)
    for m in range(STEPS):
        at = slice(m * rows, (m + 1) * rows)
        left = dot(kernel[at, :], coefs[...], ((1,), (0,))) - targets_ref[at, :].astype(F32)
        residual_ref[at, :] = left
        rounded[at, :] = left.astype(BF16)
    grad = dot(kernel[...], rounded[...], ((0,), (0,)))
    for f in range(far):
        for i, swapped in enumerate(ACROSS):
            at = (f * len(ACROSS) + i) * each
            here, there = grad[at : at + each], grad[half + at : half + at + each]
            kept_ref[at : at + each, :] = there if swapped else here
            sent_ref[at : at + each, :] = here if swapped else there


def write_kernel(source, target, sem):
    for copy in start_copies(source, target, sem, sem.shape[0]):
        copy.wait()


def sum_kernel(*refs):
    *parts, total_ref = [ref[...] for ref in refs[:-1]] + [refs[-1]]
    parts = parts[:1] + parts[:0:-1]
    while len(parts) > 1:
        parts = [a + b for a, b in zip(parts[: len(parts) // 2], parts[len(parts) // 2 :])]
    total_ref[...] = parts[0]


def send(x, sizes, flip, shift=0, step=1, size=1):
    blk, rep = sizes
    pairs = []
    for b in range(blk):
        for r in range(rep):
            digit = r // step % size
            pairs.append((b * rep + r, (b ^ flip) * rep + r + ((digit + shift) % size - digit) * step))
    return lax.ppermute(x, ("blk", "rep"), pairs)


def digits(size, low):
    end = size.bit_length() - 1
    return [(bit, min(bit + 2, end)) for bit in range(low, end, 2)]


def pair_sum(parts):
    while len(parts) > 1:
        parts = [parts[i] + parts[i + 1] for i in range(0, len(parts), 2)]
    return parts[0]


def per_device(sizes, point_pool, batch_rows, targets, center_pool, center_rows, coefs):
    to = functools.partial(send, sizes=sizes)
    each, outs = coefs.shape
    width = point_pool.shape[1]
    count = batch_rows.shape[0]

    rows = batch_rows.reshape(count // 128, 128)
    pool = in_hbm(point_pool)
    first = point_pool.shape[0] // 512 * 256
    piece, rows, resident = pl.pallas_call(
        piece_kernel,
        out_shape=(
            pltpu.VMEM((each, width + outs), BF16),
            pltpu.VMEM(rows.shape, rows.dtype),
            pltpu.VMEM((first, width), BF16),
        ),
        in_specs=[ANY] * 5,
        out_specs=(VMEM,) * 3,
        scratch_shapes=[
            pltpu.VMEM((1, each), jnp.int32),
            pltpu.VMEM(center_pool.shape, BF16),
            pltpu.SemaphoreType.DMA((4,)),
            pltpu.SemaphoreType.DMA((4,)),
        ],
        compiler_params=pltpu.CompilerParams(vmem_limit_bytes=8 << 20),
        name="piece",
    )(in_hbm(center_rows.reshape(1, each)), in_hbm(center_pool), in_hbm(coefs), in_hbm(rows), pool)

    chips = [[d << low for d in range(1, 1 << (high - low))] for low, high in digits(sizes[0], 1)]
    reps = digits(sizes[1], 0)
    near = [0] + chips[0]
    parts = [piece] + [to(piece, flip=d ^ across) for d, across in zip(near[1:], ACROSS[1:])]
    points, point_norm, goals = pl.pallas_call(
        points_kernel,
        out_shape=(
            pltpu.VMEM((count, width), BF16),
            pltpu.VMEM((count, 1), F32),
            pltpu.VMEM(targets.shape, BF16),
        ),
        in_specs=[VMEM, VMEM, ANY, ANY],
        out_specs=(VMEM,) * 3,
        scratch_shapes=[
            pltpu.VMEM((point_pool.shape[0] - first, width), BF16),
            pltpu.VMEM((count, point_pool.shape[0]), BF16),
            pltpu.VMEM((count, width), F32),
            pltpu.VMEM((count, 128), F32),
            pltpu.SemaphoreType.DMA((8,)),
        ],
        compiler_params=pltpu.CompilerParams(vmem_limit_bytes=32 << 20),
        cost_estimate=pl.CostEstimate(flops=2 << 30, bytes_accessed=5 << 20, transcendentals=0),
        name="points",
    )(rows, resident, pool, in_hbm(targets))
    parts, points, point_norm, goals = lax.optimization_barrier((parts, points, point_norm, goals))
    block = jnp.concatenate(parts, axis=0)
    for group in chips[1:]:
        block = jnp.concatenate([block] + [to(block, flip=d) for d in group], axis=0)
    half = block.shape[0]
    far = half // (len(near) * each)
    residual, kept, sent = pl.pallas_call(
        functools.partial(residual_kernel, far, each),
        out_shape=(
            pltpu.VMEM((count, outs), F32),
            pltpu.VMEM((half, outs), F32),
            pltpu.VMEM((half, outs), F32),
        ),
        in_specs=[VMEM] * 5,
        out_specs=(VMEM,) * 3,
        scratch_shapes=[
            pltpu.VMEM((2 * half, width), BF16),
            pltpu.VMEM((2 * half, outs), BF16),
            pltpu.VMEM((count, 2 * half), BF16),
            pltpu.VMEM((count, outs), BF16),
        ],
        compiler_params=pltpu.CompilerParams(vmem_limit_bytes=32 << 20),
        name="residual",
    )(points, point_norm, goals, block, to(block, flip=1))

    total = (kept + to(sent, flip=1)).reshape(far, len(near), each, outs)
    for group in reversed(chips[1:]):
        low = total.shape[0] // (len(group) + 1)
        blocks = [total[i * low : (i + 1) * low] for i in range(len(group) + 1)]
        total = pair_sum(blocks[:1] + [to(x, flip=d) for x, d in zip(blocks[1:], group)])
    rows = {d: total[0, i] for i, d in enumerate(near)}
    parts = [rows[0]] + [to(rows[d], flip=d ^ 1) for d in chips[0]]
    residual = pl.pallas_call(
        write_kernel,
        out_shape=jax.ShapeDtypeStruct(residual.shape, F32),
        in_specs=[VMEM],
        out_specs=ANY,
        scratch_shapes=[pltpu.SemaphoreType.DMA((4,))],
        compiler_params=pltpu.CompilerParams(vmem_limit_bytes=8 << 20),
        cost_estimate=pl.CostEstimate(flops=0, bytes_accessed=4 << 20, transcendentals=0),
        name="write",
    )(residual)
    parts, residual = lax.optimization_barrier((parts, residual))
    mine = pair_sum(parts)
    flip = 1
    for low, high in reps:
        size = 1 << (high - low)
        around = [to(mine, flip=flip, shift=k, step=1 << low, size=size) for k in range(1, size)]
        mine = pl.pallas_call(
            sum_kernel,
            out_shape=jax.ShapeDtypeStruct(mine.shape, F32),
            in_specs=[VMEM] * size,
            out_specs=VMEM,
            compiler_params=pltpu.CompilerParams(vmem_limit_bytes=4 << 20),
            name="sum",
        )(to(mine, flip=1) if flip else mine, *around[::-1])
        flip = 0
    return residual, mine


def solution(mesh):
    return jax.shard_map(
        functools.partial(per_device, (mesh.shape["blk"], mesh.shape["rep"])),
        mesh=mesh,
        in_specs=(
            P(("blk", "rep"), None),
            P(("blk", "rep")),
            P(("blk", "rep"), None),
            P("blk", None),
            P("blk"),
            P("blk", None),
        ),
        out_specs=(P(("blk", "rep"), None), P("blk", None)),
        check_vma=False,
    )
```

```python
import functools

import jax
import jax.numpy as jnp
from jax import lax
from jax.experimental import pallas as pl
from jax.experimental.pallas import tpu as pltpu
from jax.sharding import PartitionSpec as P

F32, BF16 = jnp.float32, jnp.bfloat16
STEPS = 2
VMEM = pl.BlockSpec(memory_space=pltpu.VMEM)
ANY = pl.BlockSpec(memory_space=pl.ANY)


def in_hbm(x):
    return pltpu.with_memory_space_constraint(x, pltpu.HBM)


def dot(a, b, contract):
    return lax.dot_general(a, b, (contract, ((), ())), preferred_element_type=F32)


def start_copies(source, target, sem, parts):
    step = source.shape[0] // parts
    copies = []
    for p in range(parts):
        at = slice(p * step, (p + 1) * step)
        copies.append(pltpu.make_async_copy(source.at[at, :], target.at[at, :], sem.at[p]))
        copies[-1].start()
    return copies


def piece_kernel(rows_hbm, centers_hbm, coefs_hbm, picks_hbm, pool_hbm, piece_ref, picks_ref, pool_ref, rows_ref, centers_ref, sem, pool_sem):
    candidates, width = centers_ref.shape
    copies = [
        pltpu.make_async_copy(rows_hbm, rows_ref, sem.at[0]),
        pltpu.make_async_copy(centers_hbm, centers_ref, sem.at[1]),
        pltpu.make_async_copy(coefs_hbm, piece_ref.at[:, width:], sem.at[2]),
        pltpu.make_async_copy(picks_hbm, picks_ref, sem.at[3]),
    ]
    for copy in copies:
        copy.start()
    first = pool_ref.shape[0]
    copies += start_copies(pool_hbm.at[:first, :], pool_ref, pool_sem, pool_sem.shape[0])
    copies[0].wait()
    picked = lax.broadcasted_iota(jnp.int32, (candidates, rows_ref.shape[1]), 0) == rows_ref[...]
    picked = picked.astype(F32).astype(BF16)
    copies[1].wait()
    piece_ref[:, :width] = dot(picked, centers_ref[...], ((0,), (0,))).astype(BF16)
    for copy in copies[2:]:
        copy.wait()


def points_kernel(rows_ref, first_ref, pool_hbm, targets_hbm, points_ref, norm_ref, targets_ref, rest_ref, picks, partial, squares, sem):
    first, width = first_ref.shape
    count = first + rest_ref.shape[0]
    parts = sem.shape[0] // 2
    copies = start_copies(pool_hbm.at[first:, :], rest_ref, sem, parts)
    later = start_copies(targets_hbm, targets_ref, sem.at[parts:], parts)
    lane = lax.broadcasted_iota(jnp.int32, (128, 128), 1).astype(jnp.int16)
    one, zero = jnp.ones((128, 128), BF16), jnp.zeros((128, 128), BF16)
    for j in range(rows_ref.shape[0]):
        row = jnp.broadcast_to(rows_ref[j : j + 1, :], (128, 128)).T.astype(jnp.int16)
        for g in range(count // 128):
            picks[j * 128 : (j + 1) * 128, g * 128 : (g + 1) * 128] = (
                jnp.where(row == lane + jnp.int16(g * 128), one, zero)
            )
    for n in range(width // 256):
        at = slice(n * 256, (n + 1) * 256)
        partial[:, at] = dot(picks[:, :first], first_ref[:, at], ((1,), (0,)))
    for copy in copies:
        copy.wait()
    for n in range(width // 256):
        at = slice(n * 256, (n + 1) * 256)
        block = partial[:, at] + dot(picks[:, first:], rest_ref[:, at], ((1,), (0,)))
        points_ref[:, at] = block.astype(BF16)
        square = block[:, :128] * block[:, :128] + block[:, 128:] * block[:, 128:]
        squares[...] = square if n == 0 else squares[...] + square
    norm_ref[...] = jnp.sum(squares[...], axis=1, keepdims=True)
    for copy in later:
        copy.wait()


def residual_kernel(far, each, points_ref, norm_ref, targets_ref, own_ref, other_ref, residual_ref, kept_ref, sent_ref, centers, coefs, kernel, rounded):
    half = own_ref.shape[0]
    count, width = points_ref.shape
    for i, ref in enumerate((own_ref, other_ref)):
        centers[i * half : (i + 1) * half, :] = ref[:, :width]
        coefs[i * half : (i + 1) * half, :] = ref[:, width:]
    squares = jnp.zeros((2 * half, 128), F32)
    for g in range(width // 128):
        part = centers[:, g * 128 : (g + 1) * 128].astype(F32)
        squares = squares + part * part
    center_norm = jnp.sum(squares.T, axis=0, keepdims=True)
    rows = count // STEPS
    for m in range(STEPS):
        at = slice(m * rows, (m + 1) * rows)
        inner = dot(points_ref[at, :], centers[...], ((1,), (1,)))
        distance = norm_ref[at, :] + center_norm - 2.0 * inner
        kernel[at, :] = jnp.exp(distance * (-1.0 / width)).astype(BF16)
    for m in range(STEPS):
        at = slice(m * rows, (m + 1) * rows)
        left = dot(kernel[at, :], coefs[...], ((1,), (0,))) - targets_ref[at, :].astype(F32)
        residual_ref[at, :] = left
        rounded[at, :] = left.astype(BF16)
    grad = dot(kernel[...], rounded[...], ((0,), (0,)))
    even = lax.rem(lax.axis_index("blk"), 2) == 0
    step = half // far
    for f in range(far):
        own, first, second, last, other, third, fourth, final = (
            grad[at + i * each : at + (i + 1) * each] for at in (f * step, half + f * step) for i in range(4)
        )
        kept = other, jnp.where(even, third, fourth), jnp.where(even, fourth, third), last
        sent = own, jnp.where(even, second, first), jnp.where(even, first, second), final
        for i in range(4):
            at = f * step + i * each
            kept_ref[at : at + each, :] = kept[i]
            sent_ref[at : at + each, :] = sent[i]


def write_kernel(source, target, sem):
    for copy in start_copies(source, target, sem, sem.shape[0]):
        copy.wait()


def sum_kernel(*refs):
    *parts, total_ref = [ref[...] for ref in refs[:-1]] + [refs[-1]]
    parts = parts[:1] + parts[:0:-1]
    while len(parts) > 1:
        parts = [a + b for a, b in zip(parts[: len(parts) // 2], parts[len(parts) // 2 :])]
    total_ref[...] = parts[0]


def send(x, sizes, flip, shift=0, step=1, size=1):
    blk, rep = sizes
    flips = flip if isinstance(flip, tuple) else (flip, flip)
    pairs = []
    for b in range(blk):
        for r in range(rep):
            digit = r // step % size
            pairs.append((b * rep + r, (b ^ flips[b % 2]) * rep + r + ((digit + shift) % size - digit) * step))
    return lax.ppermute(x, ("blk", "rep"), pairs)


def digits(size, low):
    end = size.bit_length() - 1
    return [(bit, min(bit + 2, end)) for bit in range(low, end, 2)]


def pair_sum(parts):
    while len(parts) > 1:
        parts = [parts[i] + parts[i + 1] for i in range(0, len(parts), 2)]
    return parts[0]


def per_device(sizes, point_pool, batch_rows, targets, center_pool, center_rows, coefs):
    to = functools.partial(send, sizes=sizes)
    each, outs = coefs.shape
    width = point_pool.shape[1]
    count = batch_rows.shape[0]

    rows = batch_rows.reshape(count // 128, 128)
    pool = in_hbm(point_pool)
    first = point_pool.shape[0] // 512 * 256
    piece, rows, resident = pl.pallas_call(
        piece_kernel,
        out_shape=(
            pltpu.VMEM((each, width + outs), BF16),
            pltpu.VMEM(rows.shape, rows.dtype),
            pltpu.VMEM((first, width), BF16),
        ),
        in_specs=[ANY] * 5,
        out_specs=(VMEM,) * 3,
        scratch_shapes=[
            pltpu.VMEM((1, each), jnp.int32),
            pltpu.VMEM(center_pool.shape, BF16),
            pltpu.SemaphoreType.DMA((4,)),
            pltpu.SemaphoreType.DMA((4,)),
        ],
        compiler_params=pltpu.CompilerParams(vmem_limit_bytes=8 << 20),
        name="piece",
    )(in_hbm(center_rows.reshape(1, each)), in_hbm(center_pool), in_hbm(coefs), in_hbm(rows), pool)

    chips = [[d << low for d in range(1, 1 << (high - low))] for low, high in digits(sizes[0], 1)]
    reps = digits(sizes[1], 0)
    across, along, diagonal = chips[0]
    parts = [
        piece,
        to(piece, flip=(across ^ 1, along ^ 1)),
        to(piece, flip=(along ^ 1, across ^ 1)),
        to(piece, flip=diagonal),
    ]
    points, point_norm, goals = pl.pallas_call(
        points_kernel,
        out_shape=(
            pltpu.VMEM((count, width), BF16),
            pltpu.VMEM((count, 1), F32),
            pltpu.VMEM(targets.shape, BF16),
        ),
        in_specs=[VMEM, VMEM, ANY, ANY],
        out_specs=(VMEM,) * 3,
        scratch_shapes=[
            pltpu.VMEM((point_pool.shape[0] - first, width), BF16),
            pltpu.VMEM((count, point_pool.shape[0]), BF16),
            pltpu.VMEM((count, width), F32),
            pltpu.VMEM((count, 128), F32),
            pltpu.SemaphoreType.DMA((8,)),
        ],
        compiler_params=pltpu.CompilerParams(vmem_limit_bytes=32 << 20),
        cost_estimate=pl.CostEstimate(flops=2 << 30, bytes_accessed=5 << 20, transcendentals=0),
        name="points",
    )(rows, resident, pool, in_hbm(targets))
    parts, points, point_norm, goals = lax.optimization_barrier((parts, points, point_norm, goals))
    block = jnp.concatenate(parts, axis=0)
    for group in chips[1:]:
        block = jnp.concatenate([block] + [to(block, flip=d) for d in group], axis=0)
    half = block.shape[0]
    far = half // (len(parts) * each)
    residual, kept, sent = pl.pallas_call(
        functools.partial(residual_kernel, far, each),
        out_shape=(
            pltpu.VMEM((count, outs), F32),
            pltpu.VMEM((half, outs), F32),
            pltpu.VMEM((half, outs), F32),
        ),
        in_specs=[VMEM] * 5,
        out_specs=(VMEM,) * 3,
        scratch_shapes=[
            pltpu.VMEM((2 * half, width), BF16),
            pltpu.VMEM((2 * half, outs), BF16),
            pltpu.VMEM((count, 2 * half), BF16),
            pltpu.VMEM((count, outs), BF16),
        ],
        compiler_params=pltpu.CompilerParams(vmem_limit_bytes=32 << 20),
        name="residual",
    )(points, point_norm, goals, block, to(block, flip=1))

    total = (kept + to(sent, flip=1)).reshape(far, len(parts), each, outs)
    for group in reversed(chips[1:]):
        low = total.shape[0] // (len(group) + 1)
        blocks = [total[i * low : (i + 1) * low] for i in range(len(group) + 1)]
        total = pair_sum(blocks[:1] + [to(x, flip=d) for x, d in zip(blocks[1:], group)])
    mine, *others = total[0]
    parts = [mine] + [to(x, flip=d ^ 1) for x, d in zip(others, chips[0])]
    residual = pl.pallas_call(
        write_kernel,
        out_shape=jax.ShapeDtypeStruct(residual.shape, F32),
        in_specs=[VMEM],
        out_specs=ANY,
        scratch_shapes=[pltpu.SemaphoreType.DMA((4,))],
        compiler_params=pltpu.CompilerParams(vmem_limit_bytes=8 << 20),
        cost_estimate=pl.CostEstimate(flops=0, bytes_accessed=4 << 20, transcendentals=0),
        name="write",
    )(residual)
    parts, residual = lax.optimization_barrier((parts, residual))
    mine = pair_sum(parts)
    flip = 1
    for low, high in reps:
        size = 1 << (high - low)
        around = [to(mine, flip=flip, shift=k, step=1 << low, size=size) for k in range(1, size)]
        mine = pl.pallas_call(
            sum_kernel,
            out_shape=jax.ShapeDtypeStruct(mine.shape, F32),
            in_specs=[VMEM] * size,
            out_specs=VMEM,
            compiler_params=pltpu.CompilerParams(vmem_limit_bytes=4 << 20),
            name="sum",
        )(to(mine, flip=1) if flip else mine, *around[::-1])
        flip = 0
    return residual, mine


def solution(mesh):
    return jax.shard_map(
        functools.partial(per_device, (mesh.shape["blk"], mesh.shape["rep"])),
        mesh=mesh,
        in_specs=(
            P(("blk", "rep"), None),
            P(("blk", "rep")),
            P(("blk", "rep"), None),
            P("blk", None),
            P("blk"),
            P("blk", None),
        ),
        out_specs=(P(("blk", "rep"), None), P("blk", None)),
        check_vma=False,
    )
```

```python
import functools

import jax
import jax.numpy as jnp
from jax import lax
from jax.experimental import pallas as pl
from jax.experimental.pallas import tpu as pltpu
from jax.sharding import PartitionSpec as P

F32, BF16 = jnp.float32, jnp.bfloat16
STEPS = 2
VMEM = pl.BlockSpec(memory_space=pltpu.VMEM)
ANY = pl.BlockSpec(memory_space=pl.ANY)


def in_hbm(x):
    return pltpu.with_memory_space_constraint(x, pltpu.HBM)


def dot(a, b, contract):
    return lax.dot_general(a, b, (contract, ((), ())), preferred_element_type=F32)


def start_copies(source, target, sem, parts):
    step = source.shape[0] // parts
    copies = []
    for p in range(parts):
        at = slice(p * step, (p + 1) * step)
        copies.append(pltpu.make_async_copy(source.at[at, :], target.at[at, :], sem.at[p]))
        copies[-1].start()
    return copies


def piece_kernel(rows_hbm, centers_hbm, coefs_hbm, picks_hbm, pool_hbm, piece_ref, picks_ref, pool_ref, rows_ref, centers_ref, sem, pool_sem):
    candidates, width = centers_ref.shape
    copies = [
        pltpu.make_async_copy(rows_hbm, rows_ref, sem.at[0]),
        pltpu.make_async_copy(centers_hbm, centers_ref, sem.at[1]),
        pltpu.make_async_copy(coefs_hbm, piece_ref.at[:, width:], sem.at[2]),
        pltpu.make_async_copy(picks_hbm, picks_ref, sem.at[3]),
    ]
    for copy in copies:
        copy.start()
    first = pool_ref.shape[0]
    copies += start_copies(pool_hbm.at[:first, :], pool_ref, pool_sem, pool_sem.shape[0])
    copies[0].wait()
    picked = lax.broadcasted_iota(jnp.int32, (candidates, rows_ref.shape[1]), 0) == rows_ref[...]
    picked = picked.astype(F32).astype(BF16)
    copies[1].wait()
    piece_ref[:, :width] = dot(picked, centers_ref[...], ((0,), (0,))).astype(BF16)
    for copy in copies[2:]:
        copy.wait()


def points_kernel(rows_ref, first_ref, pool_hbm, targets_hbm, points_ref, norm_ref, targets_ref, rest_ref, picks, partial, squares, sem):
    first, width = first_ref.shape
    count = first + rest_ref.shape[0]
    parts = sem.shape[0] // 2
    copies = start_copies(pool_hbm.at[first:, :], rest_ref, sem, parts)
    later = start_copies(targets_hbm, targets_ref, sem.at[parts:], parts)
    lane = lax.broadcasted_iota(jnp.int32, (128, 128), 1).astype(jnp.int16)
    one, zero = jnp.ones((128, 128), BF16), jnp.zeros((128, 128), BF16)
    for j in range(rows_ref.shape[0]):
        row = jnp.broadcast_to(rows_ref[j : j + 1, :], (128, 128)).T.astype(jnp.int16)
        for g in range(count // 128):
            picks[j * 128 : (j + 1) * 128, g * 128 : (g + 1) * 128] = (
                jnp.where(row == lane + jnp.int16(g * 128), one, zero)
            )
    for n in range(width // 256):
        at = slice(n * 256, (n + 1) * 256)
        partial[:, at] = dot(picks[:, :first], first_ref[:, at], ((1,), (0,)))
    for copy in copies:
        copy.wait()
    for n in range(width // 256):
        at = slice(n * 256, (n + 1) * 256)
        block = partial[:, at] + dot(picks[:, first:], rest_ref[:, at], ((1,), (0,)))
        points_ref[:, at] = block.astype(BF16)
        square = block[:, :128] * block[:, :128] + block[:, 128:] * block[:, 128:]
        squares[...] = square if n == 0 else squares[...] + square
    norm_ref[...] = jnp.sum(squares[...], axis=1, keepdims=True)
    for copy in later:
        copy.wait()


def residual_kernel(far, each, blocks, points_ref, norm_ref, targets_ref, *refs):
    residual_ref, kept_ref, sent_ref, centers, coefs, kernel, rounded = refs[blocks:]
    half = kept_ref.shape[0]
    count, width = points_ref.shape
    start = 0
    for ref in refs[:blocks]:
        at = slice(start, start + ref.shape[0])
        centers[at, :] = ref[:, :width]
        coefs[at, :] = ref[:, width:]
        start += ref.shape[0]
    squares = jnp.zeros((2 * half, 128), F32)
    for g in range(width // 128):
        part = centers[:, g * 128 : (g + 1) * 128].astype(F32)
        squares = squares + part * part
    center_norm = jnp.sum(squares.T, axis=0, keepdims=True)
    rows = count // STEPS
    for m in range(STEPS):
        at = slice(m * rows, (m + 1) * rows)
        inner = dot(points_ref[at, :], centers[...], ((1,), (1,)))
        distance = norm_ref[at, :] + center_norm - 2.0 * inner
        kernel[at, :] = jnp.exp(distance * (-1.0 / width)).astype(BF16)
    for m in range(STEPS):
        at = slice(m * rows, (m + 1) * rows)
        left = dot(kernel[at, :], coefs[...], ((1,), (0,))) - targets_ref[at, :].astype(F32)
        residual_ref[at, :] = left
        rounded[at, :] = left.astype(BF16)
    grad = dot(kernel[...], rounded[...], ((0,), (0,)))
    even = lax.rem(lax.axis_index("blk"), 2) == 0
    step = half // far
    for f in range(far):
        own, first, second, last, other, third, fourth, final = (
            grad[at + i * each : at + (i + 1) * each] for at in (f * step, half + f * step) for i in range(4)
        )
        kept = other, jnp.where(even, third, fourth), jnp.where(even, fourth, third), last
        sent = own, jnp.where(even, second, first), jnp.where(even, first, second), final
        for i in range(4):
            at = f * step + i * each
            kept_ref[at : at + each, :] = kept[i]
            sent_ref[at : at + each, :] = sent[i]


def write_kernel(source, target, sem):
    for copy in start_copies(source, target, sem, sem.shape[0]):
        copy.wait()


def sum_kernel(*refs):
    *parts, total_ref = [ref[...] for ref in refs[:-1]] + [refs[-1]]
    parts = parts[:1] + parts[:0:-1]
    while len(parts) > 1:
        parts = [a + b for a, b in zip(parts[: len(parts) // 2], parts[len(parts) // 2 :])]
    total_ref[...] = parts[0]


def send(x, sizes, flip, shift=0, step=1, size=1):
    blk, rep = sizes
    flips = flip if isinstance(flip, tuple) else (flip, flip)
    pairs = []
    for b in range(blk):
        for r in range(rep):
            digit = r // step % size
            pairs.append((b * rep + r, (b ^ flips[b % 2]) * rep + r + ((digit + shift) % size - digit) * step))
    return lax.ppermute(x, ("blk", "rep"), pairs)


def digits(size, low):
    end = size.bit_length() - 1
    return [(bit, min(bit + 2, end)) for bit in range(low, end, 2)]


def pair_sum(parts):
    while len(parts) > 1:
        parts = [parts[i] + parts[i + 1] for i in range(0, len(parts), 2)]
    return parts[0]


def per_device(sizes, point_pool, batch_rows, targets, center_pool, center_rows, coefs):
    to = functools.partial(send, sizes=sizes)
    each, outs = coefs.shape
    width = point_pool.shape[1]
    count = batch_rows.shape[0]

    rows = batch_rows.reshape(count // 128, 128)
    pool = in_hbm(point_pool)
    first = point_pool.shape[0] // 512 * 256
    piece, rows, resident = pl.pallas_call(
        piece_kernel,
        out_shape=(
            pltpu.VMEM((each, width + outs), BF16),
            pltpu.VMEM(rows.shape, rows.dtype),
            pltpu.VMEM((first, width), BF16),
        ),
        in_specs=[ANY] * 5,
        out_specs=(VMEM,) * 3,
        scratch_shapes=[
            pltpu.VMEM((1, each), jnp.int32),
            pltpu.VMEM(center_pool.shape, BF16),
            pltpu.SemaphoreType.DMA((4,)),
            pltpu.SemaphoreType.DMA((4,)),
        ],
        compiler_params=pltpu.CompilerParams(vmem_limit_bytes=8 << 20),
        name="piece",
    )(in_hbm(center_rows.reshape(1, each)), in_hbm(center_pool), in_hbm(coefs), in_hbm(rows), pool)

    chips = [[d << low for d in range(1, 1 << (high - low))] for low, high in digits(sizes[0], 1)]
    reps = digits(sizes[1], 0)
    across, along, diagonal = chips[0]
    parts = [
        piece,
        to(piece, flip=(across ^ 1, along ^ 1)),
        to(piece, flip=(along ^ 1, across ^ 1)),
        to(piece, flip=diagonal),
    ]
    other = to(piece, flip=1)
    points, point_norm, goals = pl.pallas_call(
        points_kernel,
        out_shape=(
            pltpu.VMEM((count, width), BF16),
            pltpu.VMEM((count, 1), F32),
            pltpu.VMEM(targets.shape, BF16),
        ),
        in_specs=[VMEM, VMEM, ANY, ANY],
        out_specs=(VMEM,) * 3,
        scratch_shapes=[
            pltpu.VMEM((point_pool.shape[0] - first, width), BF16),
            pltpu.VMEM((count, point_pool.shape[0]), BF16),
            pltpu.VMEM((count, width), F32),
            pltpu.VMEM((count, 128), F32),
            pltpu.SemaphoreType.DMA((8,)),
        ],
        compiler_params=pltpu.CompilerParams(vmem_limit_bytes=32 << 20),
        cost_estimate=pl.CostEstimate(flops=2 << 30, bytes_accessed=5 << 20, transcendentals=0),
        name="points",
    )(rows, resident, pool, in_hbm(targets))
    other, parts, points, point_norm, goals = lax.optimization_barrier((other, parts, points, point_norm, goals))
    own = [parts[0], jnp.concatenate(parts[1:], axis=0)]
    others = [other, to(own[1], flip=1)]
    for group in chips[1:]:
        own, others = (
            [jnp.concatenate(blocks + [to(block, flip=d) for d in group for block in blocks], axis=0)]
            for blocks in (own, others)
        )
    blocks = own + others
    half = sum(block.shape[0] for block in own)
    far = half // (len(parts) * each)
    residual, kept, sent = pl.pallas_call(
        functools.partial(residual_kernel, far, each, len(blocks)),
        out_shape=(
            pltpu.VMEM((count, outs), F32),
            pltpu.VMEM((half, outs), F32),
            pltpu.VMEM((half, outs), F32),
        ),
        in_specs=[VMEM] * (3 + len(blocks)),
        out_specs=(VMEM,) * 3,
        scratch_shapes=[
            pltpu.VMEM((2 * half, width), BF16),
            pltpu.VMEM((2 * half, outs), BF16),
            pltpu.VMEM((count, 2 * half), BF16),
            pltpu.VMEM((count, outs), BF16),
        ],
        compiler_params=pltpu.CompilerParams(vmem_limit_bytes=32 << 20),
        name="residual",
    )(points, point_norm, goals, *blocks)

    total = (kept + to(sent, flip=1)).reshape(far, len(parts), each, outs)
    for group in reversed(chips[1:]):
        low = total.shape[0] // (len(group) + 1)
        blocks = [total[i * low : (i + 1) * low] for i in range(len(group) + 1)]
        total = pair_sum(blocks[:1] + [to(x, flip=d) for x, d in zip(blocks[1:], group)])
    mine, *others = total[0]
    parts = [mine] + [to(x, flip=d ^ 1) for x, d in zip(others, chips[0])]
    residual = pl.pallas_call(
        write_kernel,
        out_shape=jax.ShapeDtypeStruct(residual.shape, F32),
        in_specs=[VMEM],
        out_specs=ANY,
        scratch_shapes=[pltpu.SemaphoreType.DMA((4,))],
        compiler_params=pltpu.CompilerParams(vmem_limit_bytes=8 << 20),
        cost_estimate=pl.CostEstimate(flops=0, bytes_accessed=4 << 20, transcendentals=0),
        name="write",
    )(residual)
    parts, residual = lax.optimization_barrier((parts, residual))
    mine = pair_sum(parts)
    flip = 1
    for low, high in reps:
        size = 1 << (high - low)
        around = [to(mine, flip=flip, shift=k, step=1 << low, size=size) for k in range(1, size)]
        mine = pl.pallas_call(
            sum_kernel,
            out_shape=jax.ShapeDtypeStruct(mine.shape, F32),
            in_specs=[VMEM] * size,
            out_specs=VMEM,
            compiler_params=pltpu.CompilerParams(vmem_limit_bytes=4 << 20),
            name="sum",
        )(to(mine, flip=1) if flip else mine, *around[::-1])
        flip = 0
    return residual, mine


def solution(mesh):
    return jax.shard_map(
        functools.partial(per_device, (mesh.shape["blk"], mesh.shape["rep"])),
        mesh=mesh,
        in_specs=(
            P(("blk", "rep"), None),
            P(("blk", "rep")),
            P(("blk", "rep"), None),
            P("blk", None),
            P("blk"),
            P("blk", None),
        ),
        out_specs=(P(("blk", "rep"), None), P("blk", None)),
        check_vma=False,
    )
```

```python
import functools

import jax
import jax.numpy as jnp
from jax import lax
from jax.experimental import pallas as pl
from jax.experimental.pallas import tpu as pltpu
from jax.sharding import PartitionSpec as P

F32, BF16 = jnp.float32, jnp.bfloat16
STEPS = 2
VMEM = pl.BlockSpec(memory_space=pltpu.VMEM)
ANY = pl.BlockSpec(memory_space=pl.ANY)


def in_hbm(x):
    return pltpu.with_memory_space_constraint(x, pltpu.HBM)


def dot(a, b, contract):
    return lax.dot_general(a, b, (contract, ((), ())), preferred_element_type=F32)


def start_copies(source, target, sem, parts):
    step = source.shape[0] // parts
    copies = []
    for p in range(parts):
        at = slice(p * step, (p + 1) * step)
        copies.append(pltpu.make_async_copy(source.at[at, :], target.at[at, :], sem.at[p]))
        copies[-1].start()
    return copies


def piece_kernel(rows_hbm, centers_hbm, coefs_hbm, picks_hbm, pool_hbm, piece_ref, picks_ref, pool_ref, rows_ref, centers_ref, sem, pool_sem):
    candidates, width = centers_ref.shape
    copies = [
        pltpu.make_async_copy(rows_hbm, rows_ref, sem.at[0]),
        pltpu.make_async_copy(centers_hbm, centers_ref, sem.at[1]),
        pltpu.make_async_copy(coefs_hbm, piece_ref.at[:, width:], sem.at[2]),
        pltpu.make_async_copy(picks_hbm, picks_ref, sem.at[3]),
    ]
    for copy in copies:
        copy.start()
    first = pool_ref.shape[0]
    copies += start_copies(pool_hbm.at[:first, :], pool_ref, pool_sem, pool_sem.shape[0])
    copies[0].wait()
    picked = lax.broadcasted_iota(jnp.int32, (candidates, rows_ref.shape[1]), 0) == rows_ref[...]
    picked = picked.astype(F32).astype(BF16)
    copies[1].wait()
    piece_ref[:, :width] = dot(picked, centers_ref[...], ((0,), (0,))).astype(BF16)
    for copy in copies[2:]:
        copy.wait()


def points_kernel(rows_ref, first_ref, pool_hbm, targets_hbm, points_ref, norm_ref, targets_ref, rest_ref, picks, partial, squares, sem):
    first, width = first_ref.shape
    count = first + rest_ref.shape[0]
    parts = sem.shape[0] // 2
    copies = start_copies(pool_hbm.at[first:, :], rest_ref, sem, parts)
    later = start_copies(targets_hbm, targets_ref, sem.at[parts:], parts)
    lane = lax.broadcasted_iota(jnp.int32, (128, 128), 1).astype(jnp.int16)
    one, zero = jnp.ones((128, 128), BF16), jnp.zeros((128, 128), BF16)
    for j in range(rows_ref.shape[0]):
        row = jnp.broadcast_to(rows_ref[j : j + 1, :], (128, 128)).T.astype(jnp.int16)
        for g in range(count // 128):
            picks[j * 128 : (j + 1) * 128, g * 128 : (g + 1) * 128] = (
                jnp.where(row == lane + jnp.int16(g * 128), one, zero)
            )
    for n in range(width // 256):
        at = slice(n * 256, (n + 1) * 256)
        partial[:, at] = dot(picks[:, :first], first_ref[:, at], ((1,), (0,)))
    for copy in copies:
        copy.wait()
    for n in range(width // 256):
        at = slice(n * 256, (n + 1) * 256)
        block = partial[:, at] + dot(picks[:, first:], rest_ref[:, at], ((1,), (0,)))
        points_ref[:, at] = block.astype(BF16)
        square = block[:, :128] * block[:, :128] + block[:, 128:] * block[:, 128:]
        squares[...] = square if n == 0 else squares[...] + square
    norm_ref[...] = jnp.sum(squares[...], axis=1, keepdims=True)
    for copy in later:
        copy.wait()


def residual_kernel(far, each, blocks, points_ref, norm_ref, targets_ref, *refs):
    residual_ref, kept_ref, sent_ref, centers, coefs, kernel, rounded = refs[blocks:]
    half = kept_ref.shape[0]
    count, width = points_ref.shape
    start = 0
    for ref in refs[:blocks]:
        at = slice(start, start + ref.shape[0])
        centers[at, :] = ref[:, :width]
        coefs[at, :] = ref[:, width:]
        start += ref.shape[0]
    squares = jnp.zeros((2 * half, 128), F32)
    for g in range(width // 128):
        part = centers[:, g * 128 : (g + 1) * 128].astype(F32)
        squares = squares + part * part
    center_norm = jnp.sum(squares.T, axis=0, keepdims=True)
    rows = count // STEPS
    for m in range(STEPS):
        at = slice(m * rows, (m + 1) * rows)
        inner = dot(points_ref[at, :], centers[...], ((1,), (1,)))
        distance = norm_ref[at, :] + center_norm - 2.0 * inner
        kernel[at, :] = jnp.exp(distance * (-1.0 / width)).astype(BF16)
    for m in range(STEPS):
        at = slice(m * rows, (m + 1) * rows)
        left = dot(kernel[at, :], coefs[...], ((1,), (0,))) - targets_ref[at, :].astype(F32)
        residual_ref[at, :] = left
        rounded[at, :] = left.astype(BF16)
    grad = dot(kernel[...], rounded[...], ((0,), (0,)))
    even = lax.rem(lax.axis_index("blk"), 2) == 0
    step = half // far
    for f in range(far):
        own, first, second, last, other, third, fourth, final = (
            grad[at + i * each : at + (i + 1) * each] for at in (f * step, half + f * step) for i in range(4)
        )
        kept = other, jnp.where(even, third, fourth), jnp.where(even, fourth, third), last
        sent = own, jnp.where(even, second, first), jnp.where(even, first, second), final
        for i in range(4):
            at = f * step + i * each
            kept_ref[at : at + each, :] = kept[i]
            sent_ref[at : at + each, :] = sent[i]


def write_kernel(source, target, sem):
    for copy in start_copies(source, target, sem, sem.shape[0]):
        copy.wait()


def sum_kernel(*refs):
    *parts, total_ref = [ref[...] for ref in refs[:-1]] + [refs[-1]]
    parts = parts[:1] + parts[:0:-1]
    while len(parts) > 1:
        parts = [a + b for a, b in zip(parts[: len(parts) // 2], parts[len(parts) // 2 :])]
    total_ref[...] = parts[0]


def send(x, sizes, flip, shift=0, step=1, size=1):
    blk, rep = sizes
    flips = flip if isinstance(flip, tuple) else (flip, flip)
    pairs = []
    for b in range(blk):
        for r in range(rep):
            digit = r // step % size
            pairs.append((b * rep + r, (b ^ flips[b % 2]) * rep + r + ((digit + shift) % size - digit) * step))
    return lax.ppermute(x, ("blk", "rep"), pairs)


def digits(size, low):
    end = size.bit_length() - 1
    return [(bit, min(bit + 2, end)) for bit in range(low, end, 2)]


def pair_sum(parts):
    while len(parts) > 1:
        parts = [parts[i] + parts[i + 1] for i in range(0, len(parts), 2)]
    return parts[0]


def per_device(sizes, point_pool, batch_rows, targets, center_pool, center_rows, coefs):
    to = functools.partial(send, sizes=sizes)
    each, outs = coefs.shape
    width = point_pool.shape[1]
    count = batch_rows.shape[0]

    rows = batch_rows.reshape(count // 128, 128)
    pool = in_hbm(point_pool)
    first = point_pool.shape[0] // 512 * 256
    piece, rows, resident = pl.pallas_call(
        piece_kernel,
        out_shape=(
            pltpu.VMEM((each, width + outs), BF16),
            pltpu.VMEM(rows.shape, rows.dtype),
            pltpu.VMEM((first, width), BF16),
        ),
        in_specs=[ANY] * 5,
        out_specs=(VMEM,) * 3,
        scratch_shapes=[
            pltpu.VMEM((1, each), jnp.int32),
            pltpu.VMEM(center_pool.shape, BF16),
            pltpu.SemaphoreType.DMA((4,)),
            pltpu.SemaphoreType.DMA((4,)),
        ],
        compiler_params=pltpu.CompilerParams(vmem_limit_bytes=8 << 20),
        name="piece",
    )(in_hbm(center_rows.reshape(1, each)), in_hbm(center_pool), in_hbm(coefs), in_hbm(rows), pool)

    chips = [[d << low for d in range(1, 1 << (high - low))] for low, high in digits(sizes[0], 1)]
    reps = digits(sizes[1], 0)
    across, along, diagonal = chips[0]
    parts = [
        piece,
        to(piece, flip=(across ^ 1, along ^ 1)),
        to(piece, flip=(along ^ 1, across ^ 1)),
        to(piece, flip=diagonal),
    ]
    other = to(piece, flip=1)
    points, point_norm, goals = pl.pallas_call(
        points_kernel,
        out_shape=(
            pltpu.VMEM((count, width), BF16),
            pltpu.VMEM((count, 1), F32),
            pltpu.VMEM(targets.shape, BF16),
        ),
        in_specs=[VMEM, VMEM, ANY, ANY],
        out_specs=(VMEM,) * 3,
        scratch_shapes=[
            pltpu.VMEM((point_pool.shape[0] - first, width), BF16),
            pltpu.VMEM((count, point_pool.shape[0]), BF16),
            pltpu.VMEM((count, width), F32),
            pltpu.VMEM((count, 128), F32),
            pltpu.SemaphoreType.DMA((8,)),
        ],
        compiler_params=pltpu.CompilerParams(vmem_limit_bytes=32 << 20),
        cost_estimate=pl.CostEstimate(flops=2 << 30, bytes_accessed=5 << 20, transcendentals=0),
        name="points",
    )(rows, resident, pool, in_hbm(targets))
    other, parts, points, point_norm, goals = lax.optimization_barrier((other, parts, points, point_norm, goals))
    own = [parts[0], jnp.concatenate(parts[1:], axis=0)]
    others = [other, to(own[1], flip=1)]
    for group in chips[1:]:
        own, others = (
            [jnp.concatenate(blocks + [to(block, flip=d) for d in group for block in blocks], axis=0)]
            for blocks in (own, others)
        )
    blocks = own + others
    half = sum(block.shape[0] for block in own)
    far = half // (len(parts) * each)
    residual, kept, sent = pl.pallas_call(
        functools.partial(residual_kernel, far, each, len(blocks)),
        out_shape=(
            pltpu.VMEM((count, outs), F32),
            pltpu.VMEM((half, outs), F32),
            pltpu.VMEM((half, outs), F32),
        ),
        in_specs=[VMEM] * (3 + len(blocks)),
        out_specs=(VMEM,) * 3,
        scratch_shapes=[
            pltpu.VMEM((2 * half, width), BF16),
            pltpu.VMEM((2 * half, outs), BF16),
            pltpu.VMEM((count, 2 * half), BF16),
            pltpu.VMEM((count, outs), BF16),
        ],
        compiler_params=pltpu.CompilerParams(vmem_limit_bytes=32 << 20),
        name="residual",
    )(points, point_norm, goals, *blocks)

    residual = pl.pallas_call(
        write_kernel,
        out_shape=jax.ShapeDtypeStruct(residual.shape, F32),
        in_specs=[VMEM],
        out_specs=ANY,
        scratch_shapes=[pltpu.SemaphoreType.DMA((4,))],
        compiler_params=pltpu.CompilerParams(vmem_limit_bytes=8 << 20),
        cost_estimate=pl.CostEstimate(flops=0, bytes_accessed=4 << 20, transcendentals=0),
        name="write",
    )(residual)
    got, residual = lax.optimization_barrier((to(sent, flip=1), residual))
    total = (kept + got).reshape(far, len(parts), each, outs)
    for group in reversed(chips[1:]):
        low = total.shape[0] // (len(group) + 1)
        blocks = [total[i * low : (i + 1) * low] for i in range(len(group) + 1)]
        total = pair_sum(blocks[:1] + [to(x, flip=d) for x, d in zip(blocks[1:], group)])
    mine, *others = total[0]
    parts = [mine] + [to(x, flip=d ^ 1) for x, d in zip(others, chips[0])]
    mine = pair_sum(parts)
    flip = 1
    for low, high in reps:
        size = 1 << (high - low)
        around = [to(mine, flip=flip, shift=k, step=1 << low, size=size) for k in range(1, size)]
        mine = pl.pallas_call(
            sum_kernel,
            out_shape=jax.ShapeDtypeStruct(mine.shape, F32),
            in_specs=[VMEM] * size,
            out_specs=VMEM,
            compiler_params=pltpu.CompilerParams(vmem_limit_bytes=4 << 20),
            name="sum",
        )(to(mine, flip=1) if flip else mine, *around[::-1])
        flip = 0
    return residual, mine


def solution(mesh):
    return jax.shard_map(
        functools.partial(per_device, (mesh.shape["blk"], mesh.shape["rep"])),
        mesh=mesh,
        in_specs=(
            P(("blk", "rep"), None),
            P(("blk", "rep")),
            P(("blk", "rep"), None),
            P("blk", None),
            P("blk"),
            P("blk", None),
        ),
        out_specs=(P(("blk", "rep"), None), P("blk", None)),
        check_vma=False,
    )
```
